32 devices in a mesh: sp: 4 (over x, core), ep: 8 (over z, y).
Axes of the slice: x: 2, y: 2, z: 4, core: 2. Of those that a mesh axis runs over, the one named last changes fastest.
Arguments:
- latent: bfloat16 [8, 512, 4096], P('ep', 'sp'), may hold values from -36 to 36
- attention_in: bfloat16 [8, 512, 3, 4096], P('ep', 'sp'), may hold values from -6 to 6
- out_weight: bfloat16 [4096, 4096], P('sp'), may hold values from -0.09375 to 0.09375
- modulation: float32 [4, 4096], replicated, may hold values from -4 to 4
- route_experts: int32 [8, 512, 2], P('ep', 'sp'), may hold values from 0 to 15, as said below
- route_slots: int32 [8, 512, 2], P('ep', 'sp'), may hold values from 0 to 23, as said below
- route_gates: float32 [8, 512, 2], P('ep', 'sp'), may hold values from 0.1 to 1
- gate_weight: bfloat16 [8, 4096, 4096], P('ep', None, 'sp'), may hold values from -0.09375 to 0.09375
- up_weight: bfloat16 [8, 4096, 4096], P('ep', None, 'sp'), may hold values from -0.09375 to 0.09375
- down_weight: bfloat16 [8, 4096, 4096], P('ep', 'sp'), may hold values from -0.125 to 0.125
Outputs:
- block_out: bfloat16 [8, 512, 4096], P('ep', 'sp')
The draws below stay inside these ranges and needn't reach their ends.
Inputs may be any that keep to these rules, and one draw needn't show every extreme that they name: `route_experts`: each token names two different experts. Among the 128 tokens of one device block no expert is named more than 24 times; in every device block some expert is named exactly 24 times, and one expert is named exactly 24 times in every device block. `route_slots`: the routes of one device block to one expert hold distinct slots.
All inputs are finite; a program needn't handle non-finite values.
Results may differ from the reference program's by a relative error of at most 0.013.
Values may be sent and summed in bfloat16 or wider, within the bound.
No kernel may reach another device: no remote copies, remote signals or barrier semaphores. Data moves between devices by JAX's collectives and lax.ppermute only.
A program may use at most 192 MiB of HBM per device.

```python
import math
import jax
import jax.numpy as jnp
from jax import lax

D = 4096
HD = 128
FF = 2048
TOK_DEV = 128
EXPERTS = 16
WINDOWS = 8
WIN_TOK = 512
GROUP_HEADS = 8
SHARDS = 2
SHARD_FF = 1024
CAP = 24
N_SP = 4


def route_tables(key):
    block_count = WINDOWS * (WIN_TOK // TOK_DEV)
    hot_expert = jax.random.randint(jax.random.fold_in(key, 101), (), 0, EXPERTS)
    block_keys = jax.random.split(jax.random.fold_in(key, 102), block_count)

    def one_block(block_key):
        key_order, key_count, key_slot, key_token, key_swap = jax.random.split(block_key, 5)
        ranks = jnp.arange(EXPERTS, dtype=jnp.int32)
        ordering = jax.random.permutation(key_order, EXPERTS).astype(jnp.int32)
        first_label = ordering[0]
        ordering = jnp.where(ordering == hot_expert, first_label, ordering)
        ordering = jnp.where(ranks == 0, hot_expert, ordering)
        hot_count = jax.random.randint(key_count, (), 1, 6)
        rest_total = 2 * TOK_DEV - hot_count * CAP
        others = EXPERTS - hot_count
        base_load = rest_total // others
        extra_ones = rest_total % others
        loads = jnp.where(ranks < hot_count, CAP, base_load + (ranks - hot_count < extra_ones).astype(jnp.int32))
        run_ends = jnp.cumsum(loads)
        starts = run_ends - loads
        position = jnp.arange(2 * TOK_DEV, dtype=jnp.int32)
        run_index = jnp.sum((position[:, None] >= run_ends[None, :]).astype(jnp.int32), axis=1)
        within = position - starts[run_index]
        labels = ordering[run_index]
        slot_scores = jax.random.randint(key_slot, (EXPERTS, CAP), 0, 1 << 20) * CAP + jnp.arange(CAP, dtype=jnp.int32)[None, :]
        slot_orders = jnp.argsort(slot_scores, axis=1, stable=True).astype(jnp.int32)
        slot_of = slot_orders[labels, within]
        pair_labels = jnp.stack([labels[:TOK_DEV], labels[TOK_DEV:]], axis=1)
        pair_slots = jnp.stack([slot_of[:TOK_DEV], slot_of[TOK_DEV:]], axis=1)
        swapped = jax.random.randint(key_swap, (TOK_DEV, 1), 0, 2) == 1
        pair_labels = jnp.where(swapped, pair_labels[:, ::-1], pair_labels)
        pair_slots = jnp.where(swapped, pair_slots[:, ::-1], pair_slots)
        token_order = jax.random.permutation(key_token, TOK_DEV)
        return (pair_labels[token_order], pair_slots[token_order])
    labels_all, slots_all = jax.vmap(one_block)(block_keys)
    return (labels_all.reshape(WINDOWS, WIN_TOK, 2).astype(jnp.int32), slots_all.reshape(WINDOWS, WIN_TOK, 2).astype(jnp.int32))


def draw_route_experts(key, part):
    shared = route_tables(key)
    return shared[0]


def draw_route_slots(key, part):
    shared = route_tables(key)
    return shared[1]


def draw_latent(key, part):
    key = jax.random.fold_in(key, 1)
    key_base, key_rows, key_cols = jax.random.split(key, 3)
    base_draw = jnp.clip(jax.random.normal(key_base, (WINDOWS, WIN_TOK, D), jnp.float32), -4.0, 4.0)
    row_scale = jnp.exp(jax.random.uniform(key_rows, (WINDOWS, WIN_TOK, 1), jnp.float32, math.log(0.3), math.log(3.0)))
    column_scale = jnp.exp(jax.random.uniform(key_cols, (1, 1, D), jnp.float32, math.log(0.3), math.log(3.0)))
    return (base_draw * row_scale * column_scale).astype(jnp.bfloat16)


def draw_attention_in(key, part):
    key = jax.random.fold_in(key, 2)
    key_base = jax.random.fold_in(key, 0)
    drawn = jnp.clip(jax.random.normal(key_base, (WINDOWS, WIN_TOK, 3, D), jnp.float32), -4.0, 4.0)
    return drawn.astype(jnp.bfloat16)


def shard_levels(stream_key, extent, cuts, low, high):
    def one(dim, blocks):
        steps = jax.random.uniform(jax.random.fold_in(jax.random.fold_in(stream_key, 6), dim), (blocks,), jnp.float32, low / len(cuts), high / len(cuts))
        return jnp.repeat(jnp.exp(steps), extent[dim] // blocks).reshape((-1,) + (1,) * (len(extent) - dim - 1))

    gain = one(*cuts[0])
    for cut in cuts[1:]:
        gain = gain * one(*cut)
    return gain


def gaussian(stream_key, dims, deviation, reach, cuts=(), held_as=jnp.bfloat16):
    entries = deviation * jax.random.normal(stream_key, dims, jnp.float32)
    if cuts:
        entries = entries * shard_levels(stream_key, dims, cuts, -0.22, 0.18)
    return jnp.clip(entries, -reach, reach).astype(held_as)


def setup_inputs(seed: int = 0) -> dict:
    keys = jax.random.split(jax.random.key(seed), 11)
    return {
        "latent": draw_latent(jax.random.fold_in(keys[10], 71), 0),
        "attention_in": draw_attention_in(jax.random.fold_in(keys[10], 71), 0),
        "out_weight": gaussian(keys[2], (D, D), D ** -0.5, 0.09375, ((0, 4),)),
        "modulation": gaussian(keys[3], (4, D), 1.0, 4.0, (), jnp.float32),
        "route_experts": draw_route_experts(jax.random.fold_in(keys[10], 71), 0),
        "route_slots": draw_route_slots(jax.random.fold_in(keys[10], 71), 0),
        "route_gates": jnp.clip(0.1 + 0.9 * jax.random.uniform(keys[6], (WINDOWS, WIN_TOK, 2), jnp.float32) ** shard_levels(keys[6], (WINDOWS, WIN_TOK, 2), ((0, 8), (1, 4)), -0.2, 0.2), 0.1, 1.0),
        "gate_weight": gaussian(keys[7], (EXPERTS // 2, D, 2 * FF), D ** -0.5, 0.09375, ((0, 8), (2, 4))),
        "up_weight": gaussian(keys[8], (EXPERTS // 2, D, 2 * FF), D ** -0.5, 0.09375, ((0, 8), (2, 4))),
        "down_weight": gaussian(keys[9], (EXPERTS // 2, 2 * FF, D), FF ** -0.5, 0.125, ((0, 8), (1, 4))),
    }


def reference(latent, attention_in, out_weight, modulation, route_experts, route_slots, route_gates, gate_weight, up_weight, down_weight):
    score_scale = 1.0 / math.sqrt(HD)
    group_width = GROUP_HEADS * HD

    def window(window_in):
        totals = jnp.zeros((WIN_TOK, D), jnp.float32)
        for head_group in range(N_SP):
            first = head_group * group_width
            queries = window_in[:, 0, first:first + group_width].reshape(WIN_TOK, GROUP_HEADS, HD).astype(jnp.float32)
            key_rows = window_in[:, 1, first:first + group_width].reshape(WIN_TOK, GROUP_HEADS, HD).astype(jnp.float32)
            value_rows = window_in[:, 2, first:first + group_width].reshape(WIN_TOK, GROUP_HEADS, HD).astype(jnp.float32)
            scores = jnp.einsum('qhd,khd->hqk', queries, key_rows) * score_scale
            weights = jax.nn.softmax(scores, axis=-1).astype(jnp.bfloat16)
            attended = jnp.einsum('hqk,khd->qhd', weights.astype(jnp.float32), value_rows).astype(jnp.bfloat16)
            attended = attended.reshape(WIN_TOK, group_width)
            term = jnp.dot(attended, out_weight[first:first + group_width], preferred_element_type=jnp.float32).astype(jnp.bfloat16)
            totals = totals + term.astype(jnp.float32)
        return totals
    projected = lax.map(window, attention_in)
    residual = latent.astype(jnp.float32) + modulation[0] * projected
    row_mean = lax.optimization_barrier(jnp.mean(residual, axis=-1, keepdims=True))
    centered = residual - row_mean
    variance = lax.optimization_barrier(jnp.mean(centered * centered, axis=-1, keepdims=True))
    normed = centered * lax.rsqrt(variance + 1e-06)
    moe_in = (normed * (1.0 + modulation[2]) + modulation[1]).astype(jnp.bfloat16)
    token_count = WINDOWS * WIN_TOK
    blocks = token_count // TOK_DEV
    flat_in = moe_in.reshape(token_count, D)
    padded = jnp.concatenate([flat_in, jnp.zeros((1, D), jnp.bfloat16)], axis=0)
    expert_ids = route_experts.reshape(token_count, 2).astype(jnp.int32)
    slot_ids = route_slots.reshape(token_count, 2).astype(jnp.int32)
    gate_values = route_gates.reshape(token_count, 2).astype(jnp.float32)
    token_index = jnp.broadcast_to(jnp.arange(token_count, dtype=jnp.int32)[:, None], (token_count, 2))
    block_index = token_index // TOK_DEV
    cell_index = ((expert_ids * blocks + block_index) * CAP + slot_ids).reshape(-1)
    row_table = jnp.full((EXPERTS * blocks * CAP,), token_count, jnp.int32).at[cell_index].set(token_index.reshape(-1))
    row_table = row_table.reshape(EXPERTS, blocks * CAP)
    gate_table = jnp.zeros((EXPERTS * blocks * CAP,), jnp.float32).at[cell_index].set(gate_values.reshape(-1))
    gate_table = gate_table.reshape(EXPERTS, blocks * CAP)

    def expert_step(combined, inputs):
        expert, row_index, gate_column = inputs
        rows = padded[row_index]
        pair_index = expert // 2
        half_index = expert % 2
        pair_gate = lax.dynamic_index_in_dim(gate_weight, pair_index, 0, keepdims=False)
        pair_up = lax.dynamic_index_in_dim(up_weight, pair_index, 0, keepdims=False)
        pair_down = lax.dynamic_index_in_dim(down_weight, pair_index, 0, keepdims=False)
        expert_gate = lax.dynamic_slice_in_dim(pair_gate, half_index * FF, FF, 1)
        expert_up = lax.dynamic_slice_in_dim(pair_up, half_index * FF, FF, 1)
        expert_down = lax.dynamic_slice_in_dim(pair_down, half_index * FF, FF, 0)
        output = jnp.zeros((blocks * CAP, D), jnp.float32)
        for shard_index in range(SHARDS):
            low = shard_index * SHARD_FF
            gate_part = jnp.dot(rows, expert_gate[:, low:low + SHARD_FF], preferred_element_type=jnp.float32)
            up_part = jnp.dot(rows, expert_up[:, low:low + SHARD_FF], preferred_element_type=jnp.float32)
            activation = (jax.nn.silu(gate_part) * up_part).astype(jnp.bfloat16)
            partial_value = jnp.dot(activation, expert_down[low:low + SHARD_FF], preferred_element_type=jnp.float32).astype(jnp.bfloat16)
            output = output + partial_value.astype(jnp.float32)
        combined = combined.at[row_index].add(gate_column[:, None] * output)
        return (combined, None)
    start_sum = jnp.zeros((token_count + 1, D), jnp.float32)
    combined, _ = lax.scan(expert_step, start_sum, (jnp.arange(EXPERTS, dtype=jnp.int32), row_table, gate_table))
    combined = combined[:token_count].reshape(WINDOWS, WIN_TOK, D)
    return (residual + modulation[3] * combined).astype(jnp.bfloat16)
```

```python
import functools
import math

import jax
import jax.numpy as jnp
from jax import lax
from jax.experimental import pallas as pl
from jax.experimental.pallas import tpu as pltpu
from jax.sharding import Mesh, PartitionSpec as P

HD = 128
VMEM = pl.BlockSpec(memory_space=pltpu.VMEM)
PARAMS = pltpu.CompilerParams(vmem_limit_bytes=48 * 1024 * 1024)


def dot32(a, b):
    return jnp.dot(a, b, preferred_element_type=jnp.float32)


def cost(flops, moved):
    return pl.CostEstimate(flops=int(flops), bytes_accessed=int(moved), transcendentals=0)


def attention_kernel(n_blocks, *refs):
    blocks = refs[:n_blocks]
    keep_ref, give_ref = refs[n_blocks:]
    factor = math.log2(math.e) / math.sqrt(HD)
    for head in range(keep_ref.shape[-1] // HD):
        cols = slice(head * HD, (head + 1) * HD)
        key_rows = jnp.concatenate([block[1, :, cols] for block in blocks], axis=0)
        value_rows = jnp.concatenate([block[2, :, cols] for block in blocks], axis=0)
        for i, block in enumerate(blocks):
            scores = lax.dot_general(
                block[0, :, cols],
                key_rows,
                (((1,), (1,)), ((), ())),
                preferred_element_type=jnp.float32,
            )
            lifted = jnp.exp2((scores - jnp.max(scores, axis=-1, keepdims=True)) * factor)
            total = jnp.sum(lifted, axis=-1, keepdims=True)
            mixed = dot32(lifted.astype(jnp.bfloat16), value_rows) / total
            out_ref = give_ref if i % 2 else keep_ref
            out_ref[i // 2, :, cols] = mixed.astype(jnp.bfloat16)


def attend(blocks):
    _, tokens, width = blocks[0].shape
    count = len(blocks)
    out = jax.ShapeDtypeStruct((count // 2, tokens, width), jnp.bfloat16)
    length = count * tokens
    return pl.pallas_call(
        functools.partial(attention_kernel, count),
        out_shape=(out, out),
        in_specs=[VMEM] * count,
        out_specs=(VMEM, VMEM),
        compiler_params=PARAMS,
        cost_estimate=cost(16 * length * length * width, 8 * length * width),
    )(*blocks)


def project_first_kernel(mine_ref, theirs_ref, mine_w, theirs_w, out_ref):
    n_x, tokens, width = mine_ref.shape
    mine = mine_ref[...].reshape(n_x * tokens, width)
    theirs = theirs_ref[...].reshape(n_x * tokens, width)
    out_ref[...] = dot32(mine, mine_w[...]) + dot32(theirs, theirs_w[...])


def project_first(mine, theirs, mine_w, theirs_w):
    n_x, tokens, part = mine.shape
    width = mine_w.shape[1]
    tile = min(512, width)
    rows = n_x * tokens
    whole = pl.BlockSpec((n_x, tokens, part), lambda n: (0, 0, 0))
    weight = pl.BlockSpec((part, tile), lambda n: (0, n))
    return pl.pallas_call(
        project_first_kernel,
        grid=(width // tile,),
        out_shape=jax.ShapeDtypeStruct((rows, width), jnp.float32),
        in_specs=[whole, whole, weight, weight],
        out_specs=pl.BlockSpec((rows, tile), lambda n: (0, n)),
        compiler_params=PARAMS,
        cost_estimate=cost(4 * rows * part * width, 4 * part * width + 4 * rows * width),
    )(mine, theirs, mine_w, theirs_w)


def project_last_kernel(mine_ref, theirs_ref, mine_w, theirs_w, acc_ref, own_ref, *send_refs):
    n_x, tokens, width = mine_ref.shape
    mine = mine_ref[...].reshape(n_x * tokens, width)
    theirs = theirs_ref[...].reshape(n_x * tokens, width)
    total = acc_ref[...] + dot32(mine, mine_w[...]) + dot32(theirs, theirs_w[...])
    own_ref[...] = total[:tokens]
    for i, send_ref in enumerate(send_refs):
        send_ref[...] = total[(i + 1) * tokens : (i + 2) * tokens].astype(jnp.bfloat16)


def project_last(mine, theirs, mine_w, theirs_w, acc, start, size):
    n_x, tokens, part = mine.shape
    tile = min(512, size)
    first = start // tile
    depth = mine_w.shape[0] // part - 1
    rows = n_x * tokens
    whole = pl.BlockSpec((n_x, tokens, part), lambda n: (0, 0, 0))
    weight = pl.BlockSpec((part, tile), lambda n: (depth, first + n))
    out = pl.BlockSpec((tokens, tile), lambda n: (0, n))
    return pl.pallas_call(
        project_last_kernel,
        grid=(size // tile,),
        out_shape=[jax.ShapeDtypeStruct((tokens, size), jnp.float32)]
        + [jax.ShapeDtypeStruct((tokens, size), jnp.bfloat16)] * (n_x - 1),
        in_specs=[
            whole,
            whole,
            weight,
            weight,
            pl.BlockSpec((rows, tile), lambda n: (0, first + n)),
        ],
        out_specs=[out] * n_x,
        compiler_params=PARAMS,
        cost_estimate=cost(4 * rows * part * size, 4 * part * size + 8 * rows * size),
    )(mine, theirs, mine_w, theirs_w, acc)


def norm_kernel(n_parts, n_recv, cuts, latent_ref, mod_ref, cells_ref, *refs):
    own_refs = refs[:n_parts]
    recv_refs = refs[n_parts : n_parts * (1 + n_recv)]
    residual_ref, *sent_refs = refs[n_parts * (1 + n_recv) :]
    tokens, width = latent_ref.shape
    size = width // n_parts
    sums = 0.0
    for i in range(n_parts):
        cut = slice(i * size, (i + 1) * size)
        projected = own_refs[i][...]
        for j in range(n_recv):
            projected = projected + recv_refs[i * n_recv + j][...].astype(jnp.float32)
        part = latent_ref[:, cut].astype(jnp.float32) + mod_ref[0:1, cut] * projected
        residual_ref[:, cut] = part
        sums = sums + jnp.sum(part, axis=-1, keepdims=True)
    row_mean = sums / width
    squares = 0.0
    for i in range(n_parts):
        cut = slice(i * size, (i + 1) * size)
        centered = residual_ref[:, cut] - row_mean
        squares = squares + jnp.sum(centered * centered, axis=-1, keepdims=True)
    inverse = lax.rsqrt(squares / width + 1e-06)
    cells = lax.broadcasted_iota(jnp.int32, (sent_refs[0].shape[0], tokens), 0)
    one_hot = ((cells == cells_ref[0:1, :]) | (cells == cells_ref[1:2, :])).astype(jnp.bfloat16)
    for (start, size), sent_ref in zip(cuts, sent_refs):
        cut = slice(start, start + size)
        normed = (residual_ref[:, cut] - row_mean) * inverse
        moe_in = (normed * (1.0 + mod_ref[2:3, cut]) + mod_ref[1:2, cut]).astype(jnp.bfloat16)
        sent_ref[...] = dot32(one_hot, moe_in).astype(jnp.bfloat16)


def norm_and_pack(latent, modulation, cells, n_cells, own, received, cuts):
    tokens, width = latent.shape
    flat = [piece for pieces in received for piece in pieces]
    count = 3 + len(own) + len(flat)
    return pl.pallas_call(
        functools.partial(norm_kernel, len(own), len(received[0]), cuts),
        out_shape=[jax.ShapeDtypeStruct((tokens, width), jnp.float32)]
        + [jax.ShapeDtypeStruct((n_cells, size), jnp.bfloat16) for _, size in cuts],
        in_specs=[VMEM] * count,
        out_specs=[VMEM] * (1 + len(cuts)),
        compiler_params=PARAMS,
        cost_estimate=cost(2 * n_cells * tokens * width, 20 * tokens * width),
    )(latent, modulation, cells, *own, *flat)


def ffn_in_kernel(first, last, rows_ref, *refs):
    weights, refs = refs[:4], refs[4:]
    sums = [dot32(rows_ref[...], weight[...]) for weight in weights]
    if not first:
        olds, refs = refs[:4], refs[4:]
        sums = [total + old[...] for total, old in zip(sums, olds)]
    if last:
        for gate, up, out_ref in zip(sums[:2], sums[2:], refs):
            out_ref[...] = (gate / (1.0 + jnp.exp(-gate)) * up).astype(jnp.bfloat16)
    else:
        for total, out_ref in zip(sums, refs):
            out_ref[...] = total


def ffn_in(rows, weights, olds, start, last):
    count, size = rows.shape
    units = weights[0].shape[1]
    tile = min(256, units)
    block = start // size
    weight = pl.BlockSpec((size, tile), lambda n: (block, n))
    part = pl.BlockSpec((count, tile), lambda n: (0, n))
    outs = 2 if last else 4
    kind = jnp.bfloat16 if last else jnp.float32
    return pl.pallas_call(
        functools.partial(ffn_in_kernel, not olds, last),
        grid=(units // tile,),
        out_shape=[jax.ShapeDtypeStruct((count, units), kind)] * outs,
        in_specs=[pl.BlockSpec((count, size), lambda n: (0, 0))] + [weight] * 4 + [part] * len(olds),
        out_specs=[part] * outs,
        compiler_params=PARAMS,
        cost_estimate=cost(8 * count * size * units, 8 * size * units + 16 * count * units),
    )(rows, *weights, *olds)


def ffn_out_kernel(mine_ref, theirs_ref, mine_w, theirs_w, out_ref):
    total = dot32(mine_ref[...], mine_w[...]) + dot32(theirs_ref[...], theirs_w[...])
    out_ref[...] = total.astype(jnp.bfloat16)


def ffn_out(acts, weights, start, size):
    count, units = acts[0].shape
    tile = min(512, size)
    first = start // tile
    act = pl.BlockSpec((count, units), lambda n: (0, 0))
    weight = pl.BlockSpec((units, tile), lambda n: (0, first + n))
    return pl.pallas_call(
        ffn_out_kernel,
        grid=(size // tile,),
        out_shape=jax.ShapeDtypeStruct((count, size), jnp.bfloat16),
        in_specs=[act, act, weight, weight],
        out_specs=pl.BlockSpec((count, tile), lambda n: (0, n)),
        compiler_params=PARAMS,
        cost_estimate=cost(4 * count * size * units, 4 * size * units + 2 * count * size),
    )(*acts, *weights)


def combine_kernel(residual_ref, mod_ref, cells_ref, gates_ref, back_ref, *refs):
    out_ref = refs[-1]
    tokens = residual_ref.shape[0]
    copies = back_ref.shape[1]
    n_cells = 2 * back_ref.shape[2]
    cells = lax.broadcasted_iota(jnp.int32, (tokens, n_cells), 1)
    combined = 0.0
    for route in range(2):
        one_hot = (cells == cells_ref[:, route : route + 1]).astype(jnp.bfloat16)
        picked = 0.0
        for i in range(copies):
            part = back_ref[:, i].reshape(n_cells, back_ref.shape[3])
            picked = picked + dot32(one_hot, part)
        combined = combined + gates_ref[:, route : route + 1] * picked
    out_ref[...] = (residual_ref[...] + mod_ref[3:4, :] * combined).astype(jnp.bfloat16)


def combine(residual, modulation, cells, gates, back, start, previous):
    tokens, width = residual.shape
    _, copies, half, size = back.shape
    tile = min(512, size)
    first = start // tile
    wide = pl.BlockSpec((tokens, tile), lambda n: (0, first + n))
    small = pl.BlockSpec((tokens, 2), lambda n: (0, 0))
    more = [] if previous is None else [previous]
    return pl.pallas_call(
        combine_kernel,
        grid=(size // tile,),
        out_shape=jax.ShapeDtypeStruct((tokens, width), jnp.bfloat16),
        in_specs=[
            wide,
            pl.BlockSpec((4, tile), lambda n: (0, first + n)),
            small,
            small,
            pl.BlockSpec((2, copies, half, tile), lambda n: (0, 0, 0, n)),
        ]
        + [pl.BlockSpec(memory_space=pl.ANY)] * len(more),
        out_specs=wide,
        input_output_aliases={5: 0} if more else {},
        compiler_params=PARAMS,
        cost_estimate=cost(8 * tokens * half * copies * size, 4 * half * copies * size + 6 * tokens * size),
    )(residual, modulation, cells, gates, back, *more)


def local(
    latent,
    attention_in,
    out_weight,
    modulation,
    route_experts,
    route_slots,
    route_gates,
    gate_weight,
    up_weight,
    down_weight,
):
    n_x = lax.axis_size("x")
    n_ep = lax.axis_size("ep")
    tokens = latent.shape[1]
    width = latent.shape[2]
    group_width = out_weight.shape[0]
    my_x = lax.axis_index("x")
    my_core = lax.axis_index("core")
    swap = [(0, 1), (1, 0)]
    sp_axes = ("x", "core")
    chip_axes = ("x", "ep")

    def other_core(value):
        return lax.ppermute(value, "core", swap)

    def shift(dx, dc):
        return [
            (2 * x + c, 2 * ((x + dx) % n_x) + (c ^ dc)) for x in range(n_x) for c in range(2)
        ]

    packed = jnp.transpose(attention_in[0], (1, 0, 2))
    last_part = group_width // 4
    parts = ((0, group_width - last_part), (group_width - last_part, last_part))
    pieces = []
    for start, size in parts:
        for dx in range(n_x):
            for dc in range(2):
                group = 2 * ((my_x + dx) % n_x) + (my_core ^ dc)
                pieces.append(
                    lax.dynamic_slice_in_dim(packed, group * group_width + start, size, axis=2)
                )
    blocks = []
    for i, piece in enumerate(pieces):
        dx, dc = (i // 2) % n_x, i % 2
        blocks.append(lax.ppermute(piece, sp_axes, shift(dx, dc)) if dx or dc else piece)

    out_other = other_core(out_weight)
    gates_up = (
        gate_weight[0],
        other_core(gate_weight[0]),
        up_weight[0],
        other_core(up_weight[0]),
    )
    downs = (down_weight[0], other_core(down_weight[0]))

    mine, given = attend(blocks[: 2 * n_x])
    acc = project_first(mine, other_core(given), out_weight, out_other)
    mine, given = attend(blocks[2 * n_x :])
    theirs = other_core(given)
    size = width // 2
    own, received = [], []
    for i in range(2):
        term, *sends = project_last(mine, theirs, out_weight, out_other, acc, i * size, size)
        own.append(term)
        received.append(
            [
                lax.ppermute(send, "x", [(x, (x - dx) % n_x) for x in range(n_x)])
                for dx, send in enumerate(sends, 1)
            ]
        )

    experts_count = 2 * n_ep
    capacity = max(2, 3 * tokens // experts_count)
    copies = n_x // 2
    n_cells = experts_count * capacity
    experts = route_experts[0]
    cell_index = ((experts % 2) * n_ep + experts // 2) * capacity + route_slots[0]

    cuts = ((0, 3 * width // 4), (3 * width // 4, width // 4))
    residual, *sent = norm_and_pack(
        latent[0], modulation, cell_index.T, n_cells, own, received, cuts
    )
    sums = ()
    for (start, size), part in zip(cuts, sent):
        part = jnp.broadcast_to(
            part.reshape(2, 1, n_ep, capacity, size), (2, copies, n_ep, capacity, size)
        ).reshape(n_x * n_ep, capacity, size)
        rows = lax.all_to_all(part, chip_axes, split_axis=0, concat_axis=0, tiled=True)
        sums = ffn_in(rows.reshape(-1, size), gates_up, sums, start, start + size == width)

    cuts = ((0, width // 4), (width // 4, 3 * width // 4))
    out = None
    for start, size in cuts:
        value = ffn_out(sums, downs, start, size).reshape(n_x * n_ep, capacity, size)
        back = lax.all_to_all(value, chip_axes, split_axis=0, concat_axis=0, tiled=True)
        back = back.reshape(2, copies, n_ep * capacity, size)
        out = combine(residual, modulation, cell_index, route_gates[0], back, start, out)
    return out[None]


def solution(mesh):
    n_sp, n_ep = mesh.devices.shape
    chips = Mesh(mesh.devices.reshape(n_sp // 2, 2, n_ep), ("x", "core", "ep"))
    sp = ("x", "core")
    return jax.shard_map(
        local,
        mesh=chips,
        in_specs=(
            P("ep", sp, None),
            P("ep", sp, None, None),
            P(sp, None),
            P(),
            P("ep", sp, None),
            P("ep", sp, None),
            P("ep", sp, None),
            P("ep", None, sp),
            P("ep", None, sp),
            P("ep", sp, None),
        ),
        out_specs=P("ep", sp, None),
        check_vma=False,
    )
```

```python
import functools
import math

import jax
import jax.numpy as jnp
from jax import lax
from jax.experimental import pallas as pl
from jax.experimental.pallas import tpu as pltpu
from jax.sharding import Mesh, PartitionSpec as P

HD = 128
LANES = 128
VMEM = pl.BlockSpec(memory_space=pltpu.VMEM)
LOW = pl.CostEstimate(flops=1024, bytes_accessed=1024, transcendentals=0)


def dot32(a, b):
    return jnp.dot(a, b, preferred_element_type=jnp.float32)


def grant(mebibytes):
    return pltpu.CompilerParams(vmem_limit_bytes=mebibytes * 1024 * 1024)


def after(value, token):
    return lax.optimization_barrier((value, token))[0]


FACTOR = math.log2(math.e) / math.sqrt(HD)


def score(queries, key_rows):
    return lax.dot_general(
        queries, key_rows, (((1,), (1,)), ((), ())), preferred_element_type=jnp.float32
    )


def weigh(scores, top):
    lifted = jnp.exp2((scores - top) * FACTOR)
    return lifted.astype(jnp.bfloat16), jnp.sum(lifted, axis=-1, keepdims=True)


def attend_first_kernel(*refs):
    *blocks, mixed_ref, top_ref, total_ref = refs
    for head in range(mixed_ref.shape[-1] // HD):
        cols = slice(head * HD, (head + 1) * HD)
        key_rows = jnp.concatenate([block[1, :, cols] for block in blocks], axis=0)
        value_rows = jnp.concatenate([block[2, :, cols] for block in blocks], axis=0)
        for i, block in enumerate(blocks):
            scores = score(block[0, :, cols], key_rows)
            top = jnp.max(scores, axis=-1, keepdims=True)
            weights, total = weigh(scores, top)
            mixed_ref[i, :, cols] = dot32(weights, value_rows)
            top_ref[i, :, head : head + 1] = top
            total_ref[i, :, head : head + 1] = total


def attend_first(blocks):
    _, tokens, width = blocks[0].shape
    count, heads = len(blocks), width // HD
    small = jax.ShapeDtypeStruct((count, tokens, heads), jnp.float32)
    return pl.pallas_call(
        attend_first_kernel,
        out_shape=(jax.ShapeDtypeStruct((count, tokens, width), jnp.float32), small, small),
        in_specs=[VMEM] * count,
        out_specs=(VMEM,) * 3,
        compiler_params=grant(28),
        cost_estimate=LOW,
    )(*blocks)


def attend_last_kernel(*refs):
    *blocks, mixed_ref, top_ref, total_ref, keep_ref, give_ref = refs
    last = len(blocks) - 1
    for head in range(keep_ref.shape[-1] // HD):
        cols = slice(head * HD, (head + 1) * HD)
        key_rows = jnp.concatenate([block[1, :, cols] for block in blocks], axis=0)
        value_rows = jnp.concatenate([block[2, :, cols] for block in blocks], axis=0)
        for i, block in enumerate(blocks):
            queries = block[0, :, cols]
            if i == last:
                scores = score(queries, key_rows)
                top = jnp.max(scores, axis=-1, keepdims=True)
                weights, total = weigh(scores, top)
                mixed = dot32(weights, value_rows)
            else:
                scores = score(queries, blocks[last][1, :, cols])
                old_top = top_ref[i, :, head : head + 1]
                top = jnp.maximum(old_top, jnp.max(scores, axis=-1, keepdims=True))
                scale = jnp.exp2((old_top - top) * FACTOR)
                weights, total = weigh(scores, top)
                total = total + total_ref[i, :, head : head + 1] * scale
                mixed = dot32(weights, blocks[last][2, :, cols])
                mixed = mixed + mixed_ref[i, :, cols] * scale
            out_ref = give_ref if i % 2 else keep_ref
            out_ref[i // 2, :, cols] = (mixed / total).astype(jnp.bfloat16)


def attend_last(blocks, partial_sums):
    _, tokens, width = blocks[0].shape
    count = len(blocks)
    out = jax.ShapeDtypeStruct((count // 2, tokens, width), jnp.bfloat16)
    return pl.pallas_call(
        attend_last_kernel,
        out_shape=(out, out),
        in_specs=[VMEM] * (count + 3),
        out_specs=(VMEM, VMEM),
        compiler_params=grant(28),
        cost_estimate=LOW,
    )(*blocks, *partial_sums)


def project_kernel(mine_ref, theirs_ref, mine_w, theirs_w, own_ref, *send_refs):
    n_x, tokens, width = mine_ref.shape
    mine = mine_ref[...].reshape(n_x * tokens, width)
    theirs = theirs_ref[...].reshape(n_x * tokens, width)
    total = dot32(mine, mine_w[...]) + dot32(theirs, theirs_w[...])
    own_ref[...] = total[:tokens]
    for i, send_ref in enumerate(send_refs):
        send_ref[...] = total[(i + 1) * tokens : (i + 2) * tokens].astype(jnp.bfloat16)


def project(mine, theirs, mine_w, theirs_w, start, size):
    n_x, tokens, depth = mine.shape
    tile = min(1024, size)
    first = start // tile
    whole = pl.BlockSpec((n_x, tokens, depth), lambda n: (0, 0, 0))
    weight = pl.BlockSpec((depth, tile), lambda n: (0, first + n))
    return pl.pallas_call(
        project_kernel,
        grid=(size // tile,),
        out_shape=[jax.ShapeDtypeStruct((tokens, size), jnp.float32)]
        + [jax.ShapeDtypeStruct((tokens, size), jnp.bfloat16)] * (n_x - 1),
        in_specs=[whole, whole, weight, weight],
        out_specs=[pl.BlockSpec((tokens, tile), lambda n: (0, n))] * n_x,
        compiler_params=grant(28),
        cost_estimate=LOW,
    )(mine, theirs, mine_w, theirs_w)


def residual_kernel(start, n_recv, old_size, latent_ref, mod_ref, own_ref, *refs):
    recv_refs, old_refs = refs[:n_recv], refs[n_recv:-2]
    residual_ref, stats_ref = refs[-2:]
    size = own_ref.shape[1]
    cut = slice(start, start + size)
    projected = own_ref[...]
    for recv_ref in recv_refs:
        projected = projected + recv_ref[...].astype(jnp.float32)
    part = latent_ref[:, cut].astype(jnp.float32) + mod_ref[0:1, cut] * projected
    residual_ref[...] = part
    mean = jnp.mean(part, axis=-1, keepdims=True)
    centered = part - mean
    square = jnp.sum(centered * centered, axis=-1, keepdims=True)
    for old_ref in old_refs:
        old_mean, old_square = old_ref[:, 0:1], old_ref[:, 1:2]
        gap = old_mean - mean
        width = size + old_size
        mean = mean + gap * (old_size / width)
        square = square + old_square + gap * gap * (size * old_size / width)
        square = lax.rsqrt(square / width + 1e-06)
    stats_ref[:, 0:1] = mean
    stats_ref[:, 1:2] = square


def residual_part(latent, modulation, own, received, olds, start):
    tokens, size = own.shape
    return pl.pallas_call(
        functools.partial(residual_kernel, start, len(received), start),
        out_shape=[
            jax.ShapeDtypeStruct((tokens, size), jnp.float32),
            jax.ShapeDtypeStruct((tokens, 2), jnp.float32),
        ],
        in_specs=[VMEM] * (3 + len(received) + len(olds)),
        out_specs=[VMEM] * 2,
        compiler_params=grant(28),
        cost_estimate=LOW,
    )(latent, modulation, own, *received, *olds)


def route_rows(cells_ref, sent_ref):
    tokens = cells_ref.shape[1]
    cells = lax.broadcasted_iota(jnp.int32, (sent_ref.shape[0], tokens), 0)
    return ((cells == cells_ref[0:1, :]) | (cells == cells_ref[1:2, :])).astype(jnp.bfloat16)


def pack_raw_kernel(cells_ref, part_ref, sent_ref):
    rows = part_ref[...].astype(jnp.bfloat16)
    sent_ref[...] = dot32(route_rows(cells_ref, sent_ref), rows).astype(jnp.bfloat16)


def pack_raw(cells, n_cells, part):
    return pl.pallas_call(
        pack_raw_kernel,
        out_shape=jax.ShapeDtypeStruct((n_cells, part.shape[1]), jnp.bfloat16),
        in_specs=[VMEM] * 2,
        out_specs=VMEM,
        compiler_params=grant(28),
        cost_estimate=LOW,
    )(cells, part)


def normed(part, mean, inverse, mod_ref, cut):
    rows = (part - mean) * inverse
    return (rows * (1.0 + mod_ref[2:3, cut]) + mod_ref[1:2, cut]).astype(jnp.bfloat16)


def pack_kernel(start, low, size, with_stats, mod_ref, cells_ref, stats_ref, part_ref, sent_ref):
    one_hot = route_rows(cells_ref, sent_ref)
    cut = slice(start + low, start + low + size)
    part = part_ref[:, low : low + size]
    moe_in = normed(part, stats_ref[:, 0:1], stats_ref[:, 1:2], mod_ref, cut)
    sent_ref[:, :size] = dot32(one_hot, moe_in).astype(jnp.bfloat16)
    if with_stats:
        tokens = part.shape[0]
        lane = lax.broadcasted_iota(jnp.int32, (tokens, LANES), 1)
        block = jnp.zeros((tokens, LANES), jnp.float32)
        for i in range(2):
            rest = stats_ref[:, i : i + 1]
            for j in range(3):
                piece = rest.astype(jnp.bfloat16).astype(jnp.float32)
                block = jnp.where(lane == 3 * i + j, piece, block)
                rest = rest - piece
        sent_ref[:, size:] = dot32(one_hot, block.astype(jnp.bfloat16)).astype(jnp.bfloat16)


def pack(modulation, cells, n_cells, stats, part, start, low, size, with_stats):
    wide = size + LANES if with_stats else size
    return pl.pallas_call(
        functools.partial(pack_kernel, start, low, size, with_stats),
        out_shape=jax.ShapeDtypeStruct((n_cells, wide), jnp.bfloat16),
        in_specs=[VMEM] * 4,
        out_specs=VMEM,
        compiler_params=grant(28),
        cost_estimate=LOW,
    )(modulation, cells, stats, part)


def ffn_first_kernel(mod_ref, raw_ref, rows_ref, *refs):
    weights, sums, raw_rows = refs[:4], refs[4:8], refs[8]
    size = raw_ref.shape[1]
    rest = weights[0].shape[0] - size

    @pl.when(pl.program_id(0) == 0)
    def _():
        pieces = rows_ref[:, rest : rest + LANES].astype(jnp.float32)
        mean, inverse = (
            pieces[:, i : i + 1] + pieces[:, i + 1 : i + 2] + pieces[:, i + 2 : i + 3]
            for i in (0, 3)
        )
        part = raw_ref[...].astype(jnp.float32)
        raw_rows[...] = normed(part, mean, inverse, mod_ref, slice(0, size))

    for weight, total_ref in zip(weights, sums):
        total_ref[...] = dot32(raw_rows[...], weight[:size]) + dot32(
            rows_ref[:, :rest], weight[size:]
        )


def ffn_first(modulation, raw, rows, weights):
    count, size = raw.shape
    units = weights[0].shape[1]
    tile = min(256, units)
    depth = size + rows.shape[1] - LANES
    weight = pl.BlockSpec((depth, tile), lambda n: (0, n))
    return pl.pallas_call(
        ffn_first_kernel,
        grid=(units // tile,),
        out_shape=[jax.ShapeDtypeStruct((count, units), jnp.float32)] * 4,
        in_specs=[
            pl.BlockSpec(modulation.shape, lambda n: (0, 0)),
            pl.BlockSpec(raw.shape, lambda n: (0, 0)),
            pl.BlockSpec(rows.shape, lambda n: (0, 0)),
        ]
        + [weight] * 4,
        out_specs=[pl.BlockSpec((count, tile), lambda n: (0, n))] * 4,
        scratch_shapes=[pltpu.VMEM(raw.shape, jnp.bfloat16)],
        compiler_params=grant(57),
        cost_estimate=LOW,
    )(modulation, raw, rows, *weights)


def ffn_last_kernel(rows_ref, *refs):
    weights, olds, outs = refs[:4], refs[4:8], refs[8:]
    rows = rows_ref[...]
    sums = [dot32(rows, weight[...]) + old[...] for weight, old in zip(weights, olds)]
    for gate, up, out_ref in zip(sums[:2], sums[2:], outs):
        out_ref[...] = (gate / (1.0 + jnp.exp(-gate)) * up).astype(jnp.bfloat16)


def ffn_last(rows, weights, olds):
    count, size = rows.shape
    depth, units = weights[0].shape
    tile = min(256, units)
    block = depth // size - 1
    weight = pl.BlockSpec((size, tile), lambda n: (block, n))
    part = pl.BlockSpec((count, tile), lambda n: (0, n))
    return pl.pallas_call(
        ffn_last_kernel,
        grid=(units // tile,),
        out_shape=[jax.ShapeDtypeStruct((count, units), jnp.bfloat16)] * 2,
        in_specs=[pl.BlockSpec((count, size), lambda n: (0, 0))] + [weight] * 4 + [part] * 4,
        out_specs=[part] * 2,
        compiler_params=grant(57),
        cost_estimate=LOW,
    )(rows, *weights, *olds)


def ffn_out_kernel(mine_ref, theirs_ref, mine_w, theirs_w, out_ref):
    total = dot32(mine_ref[...], mine_w[...]) + dot32(theirs_ref[...], theirs_w[...])
    out_ref[...] = total.astype(jnp.bfloat16)


def ffn_out(acts, weights, start, size):
    count, units = acts[0].shape
    tile = min(512, size)
    first = start // tile
    act = pl.BlockSpec((count, units), lambda n: (0, 0))
    weight = pl.BlockSpec((units, tile), lambda n: (0, first + n))
    return pl.pallas_call(
        ffn_out_kernel,
        grid=(size // tile,),
        out_shape=jax.ShapeDtypeStruct((count, size), jnp.bfloat16),
        in_specs=[act, act, weight, weight],
        out_specs=pl.BlockSpec((count, tile), lambda n: (0, n)),
        compiler_params=grant(57),
        cost_estimate=LOW,
    )(*acts, *weights)


def combine_kernel(residual_ref, mod_ref, cells_ref, gates_ref, back_ref, *refs):
    out_ref = refs[-1]
    tokens, tile = out_ref.shape
    _, copies, half, _ = back_ref.shape
    cells = lax.broadcasted_iota(jnp.int32, (tokens, 2 * half), 1)
    one_hot = jnp.concatenate(
        [(cells == cells_ref[:, i : i + 1]).astype(jnp.bfloat16) for i in range(2)], axis=0
    )
    picked = 0.0
    for i in range(copies):
        picked = picked + dot32(one_hot, back_ref[:, i].reshape(2 * half, tile))
    combined = gates_ref[:, 0:1] * picked[:tokens] + gates_ref[:, 1:2] * picked[tokens:]
    out_ref[...] = (residual_ref[...] + mod_ref[3:4, :] * combined).astype(jnp.bfloat16)


def combine(residual, modulation, cells, gates, back, start, previous):
    tokens, size = residual.shape
    width = modulation.shape[1]
    _, copies, half, _ = back.shape
    tile = min(1024, size)
    first = start // tile
    wide = pl.BlockSpec((tokens, tile), lambda n: (0, first + n))
    small = pl.BlockSpec((tokens, 2), lambda n: (0, 0))
    more = [] if previous is None else [previous]
    return pl.pallas_call(
        combine_kernel,
        grid=(size // tile,),
        out_shape=jax.ShapeDtypeStruct((tokens, width), jnp.bfloat16),
        in_specs=[
            pl.BlockSpec((tokens, tile), lambda n: (0, n)),
            pl.BlockSpec((4, tile), lambda n: (0, first + n)),
            small,
            small,
            pl.BlockSpec((2, copies, half, tile), lambda n: (0, 0, 0, n)),
        ]
        + [pl.BlockSpec(memory_space=pl.ANY)] * len(more),
        out_specs=wide,
        input_output_aliases={5: 0} if more else {},
        compiler_params=grant(28),
        cost_estimate=LOW,
    )(residual, modulation, cells, gates, back, *more)


def local(
    latent,
    attention_in,
    out_weight,
    modulation,
    route_experts,
    route_slots,
    route_gates,
    gate_weight,
    up_weight,
    down_weight,
):
    n_x = lax.axis_size("x")
    n_ep = lax.axis_size("ep")
    tokens = latent.shape[1]
    width = latent.shape[2]
    group_width = out_weight.shape[0]
    my_x = lax.axis_index("x")
    my_core = lax.axis_index("core")
    latent = latent[0]

    def other_core(value):
        return lax.ppermute(value, "core", [(0, 1), (1, 0)])

    def exchange(value):
        part = value.shape[-1]
        value = value.reshape(n_x * n_ep, -1, part)
        return lax.all_to_all(value, ("x", "ep"), split_axis=0, concat_axis=0, tiled=True)

    def shift(dx, dc):
        return [
            (2 * x + c, 2 * ((x + dx) % n_x) + (c ^ dc)) for x in range(n_x) for c in range(2)
        ]

    packed = jnp.transpose(attention_in[0], (1, 0, 2))
    pieces, blocks = [], []
    for dx in range(n_x):
        for dc in range(2):
            group = 2 * ((my_x + dx) % n_x) + (my_core ^ dc)
            piece = lax.dynamic_slice_in_dim(packed, group * group_width, group_width, axis=2)
            pieces.append(piece)
            if dx or dc:
                piece = lax.ppermute(piece, ("x", "core"), shift(dx, dc))
            blocks.append(piece)

    out_other = other_core(after(out_weight, pieces[1]))
    mine, given = attend_last(blocks, attend_first(blocks[:-1]))
    theirs = other_core(given)
    gate_mine, up_mine, down_mine = gate_weight[0], up_weight[0], down_weight[0]
    gate_other = other_core(after(gate_mine, theirs))
    up_other = other_core(after(up_mine, theirs))
    gates_up = (gate_mine, gate_other, up_mine, up_other)

    experts_count = 2 * n_ep
    capacity = max(2, 3 * tokens // experts_count)
    copies = n_x // 2
    n_cells = experts_count * capacity
    experts = route_experts[0]
    cells = ((experts % 2) * n_ep + experts // 2) * capacity + route_slots[0]
    row_cells = cells.T

    def dispatch(sent):
        part = sent.shape[1]
        sent = jnp.broadcast_to(
            sent.reshape(2, 1, n_ep, capacity, part), (2, copies, n_ep, capacity, part)
        )
        return exchange(sent).reshape(-1, part)

    quarter = width // 4
    cuts = ((0, quarter), (quarter, width - quarter))
    terms, received = [], []
    for start, size in cuts:
        own, *sends = project(mine, theirs, out_weight, out_other, start, size)
        mine = after(mine, own)
        if received:
            sends = after(sends, received[0])
        terms.append(own)
        received.append(
            [
                lax.ppermute(value, "x", [(x, (x - dx) % n_x) for x in range(n_x)])
                for dx, value in enumerate(sends, 1)
            ]
        )
    residual, stat = residual_part(latent, modulation, terms[0], received[0], [], 0)
    raw = pack_raw(row_cells, n_cells, residual)
    raw = dispatch(after(raw, terms[1]))
    own = after(terms[1], raw)
    rest, stats = residual_part(latent, modulation, own, received[1], [stat], quarter)
    residuals = [residual, rest]
    down_other = other_core(after(down_mine, stats))
    downs = (down_mine, down_other)

    sent = pack(modulation, row_cells, n_cells, stats, rest, quarter, 0, 2 * quarter, True)
    rows = dispatch(after(sent, raw))
    sent = pack(
        modulation, row_cells, n_cells, after(stats, sent), rest, quarter, 2 * quarter, quarter, False
    )
    last_rows = dispatch(after(sent, rows))
    sums = ffn_first(modulation, raw, rows, gates_up)
    acts = ffn_last(last_rows, gates_up, sums)

    out, token = None, acts
    for residual, (start, size) in zip(residuals, cuts):
        value = after(ffn_out(acts, downs, start, size), token)
        token = exchange(value)
        back = token.reshape(2, copies, n_ep * capacity, size)
        out = combine(residual, modulation, cells, route_gates[0], back, start, out)
    return out[None]


def solution(mesh):
    n_sp, n_ep = mesh.devices.shape
    chips = Mesh(mesh.devices.reshape(n_sp // 2, 2, n_ep), ("x", "core", "ep"))
    sp = ("x", "core")
    return jax.shard_map(
        local,
        mesh=chips,
        in_specs=(
            P("ep", sp, None),
            P("ep", sp, None, None),
            P(sp, None),
            P(),
            P("ep", sp, None),
            P("ep", sp, None),
            P("ep", sp, None),
            P("ep", None, sp),
            P("ep", None, sp),
            P("ep", sp, None),
        ),
        out_specs=P("ep", sp, None),
        check_vma=False,
    )
```

```python
import functools
import math

import jax
import jax.numpy as jnp
from jax import lax
from jax.experimental import pallas as pl
from jax.experimental.pallas import tpu as pltpu
from jax.sharding import Mesh, PartitionSpec as P

HD = 128
VMEM = pl.BlockSpec(memory_space=pltpu.VMEM)
LOW = pl.CostEstimate(flops=1024, bytes_accessed=1024, transcendentals=0)


def dot32(a, b):
    return jnp.dot(a, b, preferred_element_type=jnp.float32)


def grant(mebibytes):
    return pltpu.CompilerParams(vmem_limit_bytes=mebibytes * 1024 * 1024)


def after(value, token):
    return lax.optimization_barrier((value, token))[0]


def attention_kernel(n_blocks, *refs):
    blocks = refs[:n_blocks]
    keep_ref, give_ref = refs[n_blocks:]
    tokens = keep_ref.shape[1]
    factor = math.log2(math.e) / math.sqrt(HD)
    for head in range(keep_ref.shape[-1] // HD):
        cols = slice(head * HD, (head + 1) * HD)
        queries, key_rows, value_rows = (
            jnp.concatenate([block[i, :, cols] for block in blocks], axis=0) for i in range(3)
        )
        scores = lax.dot_general(
            queries, key_rows, (((1,), (1,)), ((), ())), preferred_element_type=jnp.float32
        )
        lifted = jnp.exp2((scores - jnp.max(scores, axis=-1, keepdims=True)) * factor)
        total = jnp.sum(lifted, axis=-1, keepdims=True)
        mixed = (dot32(lifted.astype(jnp.bfloat16), value_rows) / total).astype(jnp.bfloat16)
        for i in range(n_blocks):
            out_ref = give_ref if i % 2 else keep_ref
            out_ref[i // 2, :, cols] = mixed[i * tokens : (i + 1) * tokens]


def attend(blocks):
    _, tokens, width = blocks[0].shape
    count = len(blocks)
    out = jax.ShapeDtypeStruct((count // 2, tokens, width), jnp.bfloat16)
    return pl.pallas_call(
        functools.partial(attention_kernel, count),
        out_shape=(out, out),
        in_specs=[VMEM] * count,
        out_specs=(VMEM, VMEM),
        compiler_params=grant(28),
        cost_estimate=LOW,
    )(*blocks)


def project_kernel(mine_ref, theirs_ref, mine_w, theirs_w, *refs):
    n_x, tokens, width = mine_ref.shape
    mine = mine_ref[...].reshape(n_x * tokens, width)
    theirs = theirs_ref[...].reshape(n_x * tokens, width)
    total = dot32(mine, mine_w[...]) + dot32(theirs, theirs_w[...])

    def write(outs):
        outs[0][...] = total[:tokens]
        for i, send_ref in enumerate(outs[1:], 1):
            send_ref[...] = total[i * tokens : (i + 1) * tokens].astype(jnp.bfloat16)

    half = pl.num_programs(0) // 2

    @pl.when(pl.program_id(0) < half)
    def _():
        write(refs[:n_x])

    @pl.when(pl.program_id(0) >= half)
    def _():
        write(refs[n_x:])


def project(mine, theirs, mine_w, theirs_w):
    n_x, tokens, depth = mine.shape
    width = mine_w.shape[1]
    tile = width // 4
    whole = pl.BlockSpec((n_x, tokens, depth), lambda n: (0, 0, 0))
    weight = pl.BlockSpec((depth, tile), lambda n: (0, n))
    out_shape, out_specs = [], []
    for place in (lambda n: (0, jnp.minimum(n, 1)), lambda n: (0, jnp.maximum(n - 2, 0))):
        for i in range(n_x):
            kind = jnp.bfloat16 if i else jnp.float32
            out_shape.append(jax.ShapeDtypeStruct((tokens, width // 2), kind))
            out_specs.append(pl.BlockSpec((tokens, tile), place))
    outs = pl.pallas_call(
        project_kernel,
        grid=(4,),
        out_shape=out_shape,
        in_specs=[whole, whole, weight, weight],
        out_specs=out_specs,
        compiler_params=grant(28),
        cost_estimate=LOW,
    )(mine, theirs, mine_w, theirs_w)
    return outs[:n_x], outs[n_x:]


def residual_kernel(start, n_recv, old_size, latent_ref, mod_ref, own_ref, *refs):
    recv_refs, old_refs = refs[:n_recv], refs[n_recv:-2]
    residual_ref, stats_ref = refs[-2:]
    size = own_ref.shape[1]
    cut = slice(start, start + size)
    projected = own_ref[...]
    for recv_ref in recv_refs:
        projected = projected + recv_ref[...].astype(jnp.float32)
    part = latent_ref[:, cut].astype(jnp.float32) + mod_ref[0:1, cut] * projected
    residual_ref[...] = part
    mean = jnp.mean(part, axis=-1, keepdims=True)
    centered = part - mean
    square = jnp.sum(centered * centered, axis=-1, keepdims=True)
    for old_ref in old_refs:
        old_mean, old_square = old_ref[:, 0:1], old_ref[:, 1:2]
        gap = old_mean - mean
        width = size + old_size
        mean = mean + gap * (old_size / width)
        square = square + old_square + gap * gap * (size * old_size / width)
        square = lax.rsqrt(square / width + 1e-06)
    stats_ref[:, 0:1] = mean
    stats_ref[:, 1:2] = square


def residual_part(latent, modulation, own, received, olds, start):
    tokens, size = own.shape
    return pl.pallas_call(
        functools.partial(residual_kernel, start, len(received), start),
        out_shape=[
            jax.ShapeDtypeStruct((tokens, size), jnp.float32),
            jax.ShapeDtypeStruct((tokens, 2), jnp.float32),
        ],
        in_specs=[VMEM] * (3 + len(received) + len(olds)),
        out_specs=[VMEM] * 2,
        compiler_params=grant(28),
        cost_estimate=LOW,
    )(latent, modulation, own, *received, *olds)


def pack_kernel(start, stop, mod_ref, cells_ref, stats_ref, *refs):
    *part_refs, sent_ref = refs
    tokens, size = part_refs[0].shape
    cells = lax.broadcasted_iota(jnp.int32, (sent_ref.shape[0], tokens), 0)
    one_hot = ((cells == cells_ref[0:1, :]) | (cells == cells_ref[1:2, :])).astype(jnp.bfloat16)
    for i, part_ref in enumerate(part_refs):
        low, high = max(start, i * size), min(stop, (i + 1) * size)
        if low < high:
            cut = slice(low, high)
            part = part_ref[:, low - i * size : high - i * size]
            normed = (part - stats_ref[:, 0:1]) * stats_ref[:, 1:2]
            moe_in = (normed * (1.0 + mod_ref[2:3, cut]) + mod_ref[1:2, cut]).astype(jnp.bfloat16)
            sent_ref[:, low - start : high - start] = dot32(one_hot, moe_in).astype(jnp.bfloat16)


def pack(modulation, cells, n_cells, stats, parts, start, stop):
    return pl.pallas_call(
        functools.partial(pack_kernel, start, stop),
        out_shape=jax.ShapeDtypeStruct((n_cells, stop - start), jnp.bfloat16),
        in_specs=[VMEM] * (3 + len(parts)),
        out_specs=VMEM,
        compiler_params=grant(28),
        cost_estimate=LOW,
    )(modulation, cells, stats, *parts)


def ffn_in_kernel(first, last, rows_ref, *refs):
    weights, refs = refs[:4], refs[4:]
    sums = [dot32(rows_ref[...], weight[...]) for weight in weights]
    if not first:
        olds, refs = refs[:4], refs[4:]
        sums = [total + old[...] for total, old in zip(sums, olds)]
    if last:
        for gate, up, out_ref in zip(sums[:2], sums[2:], refs):
            out_ref[...] = (gate / (1.0 + jnp.exp(-gate)) * up).astype(jnp.bfloat16)
    else:
        for total, out_ref in zip(sums, refs):
            out_ref[...] = total


def ffn_in(rows, weights, olds, start, last):
    count, size = rows.shape
    units = weights[0].shape[1]
    tile = min(256, units)
    block = start // size
    weight = pl.BlockSpec((size, tile), lambda n: (block, n))
    part = pl.BlockSpec((count, tile), lambda n: (0, n))
    outs = 2 if last else 4
    kind = jnp.bfloat16 if last else jnp.float32
    return pl.pallas_call(
        functools.partial(ffn_in_kernel, not olds, last),
        grid=(units // tile,),
        out_shape=[jax.ShapeDtypeStruct((count, units), kind)] * outs,
        in_specs=[pl.BlockSpec((count, size), lambda n: (0, 0))] + [weight] * 4 + [part] * len(olds),
        out_specs=[part] * outs,
        compiler_params=grant(57),
        cost_estimate=LOW,
    )(rows, *weights, *olds)


def ffn_out_kernel(mine_ref, theirs_ref, mine_w, theirs_w, out_ref):
    total = dot32(mine_ref[...], mine_w[...]) + dot32(theirs_ref[...], theirs_w[...])
    out_ref[...] = total.astype(jnp.bfloat16)


def ffn_out(acts, weights, start, size):
    count, units = acts[0].shape
    tile = min(1024, size)
    first = start // tile
    act = pl.BlockSpec((count, units), lambda n: (0, 0))
    weight = pl.BlockSpec((units, tile), lambda n: (0, first + n))
    return pl.pallas_call(
        ffn_out_kernel,
        grid=(size // tile,),
        out_shape=jax.ShapeDtypeStruct((count, size), jnp.bfloat16),
        in_specs=[act, act, weight, weight],
        out_specs=pl.BlockSpec((count, tile), lambda n: (0, n)),
        compiler_params=grant(57),
        cost_estimate=LOW,
    )(*acts, *weights)


def combine_kernel(first, turn, early_ref, late_ref, mod_ref, cells_ref, gates_ref, back_ref, *refs):
    out_ref = refs[-1]
    tokens, tile = out_ref.shape
    _, copies, half, _ = back_ref.shape
    cells = lax.broadcasted_iota(jnp.int32, (tokens, 2 * half), 1)
    one_hot = jnp.concatenate(
        [(cells == cells_ref[:, i : i + 1]).astype(jnp.bfloat16) for i in range(2)], axis=0
    )
    picked = 0.0
    for i in range(copies):
        picked = picked + dot32(one_hot, back_ref[:, i].reshape(2 * half, tile))
    combined = gates_ref[:, 0:1] * picked[:tokens] + gates_ref[:, 1:2] * picked[tokens:]
    is_early = first + pl.program_id(0) < turn
    residual = jnp.where(is_early, early_ref[...], late_ref[...])
    out_ref[...] = (residual + mod_ref[3:4, :] * combined).astype(jnp.bfloat16)


def combine(residuals, modulation, cells, gates, back, start, previous):
    tokens, part = residuals[0].shape
    width = modulation.shape[1]
    _, copies, half, size = back.shape
    tile = min(1024, size)
    first, turn = start // tile, part // tile
    small = pl.BlockSpec((tokens, 2), lambda n: (0, 0))
    more = [] if previous is None else [previous]
    return pl.pallas_call(
        functools.partial(combine_kernel, first, turn),
        grid=(size // tile,),
        out_shape=jax.ShapeDtypeStruct((tokens, width), jnp.bfloat16),
        in_specs=[
            pl.BlockSpec((tokens, tile), lambda n: (0, jnp.minimum(first + n, turn - 1))),
            pl.BlockSpec((tokens, tile), lambda n: (0, jnp.maximum(first + n - turn, 0))),
            pl.BlockSpec((4, tile), lambda n: (0, first + n)),
            small,
            small,
            pl.BlockSpec((2, copies, half, tile), lambda n: (0, 0, 0, n)),
        ]
        + [pl.BlockSpec(memory_space=pl.ANY)] * len(more),
        out_specs=pl.BlockSpec((tokens, tile), lambda n: (0, first + n)),
        input_output_aliases={6: 0} if more else {},
        compiler_params=grant(28),
        cost_estimate=LOW,
    )(*residuals, modulation, cells, gates, back, *more)


def local(
    latent,
    attention_in,
    out_weight,
    modulation,
    route_experts,
    route_slots,
    route_gates,
    gate_weight,
    up_weight,
    down_weight,
):
    n_x = lax.axis_size("x")
    n_ep = lax.axis_size("ep")
    tokens = latent.shape[1]
    width = latent.shape[2]
    group_width = out_weight.shape[0]
    my_x = lax.axis_index("x")
    my_core = lax.axis_index("core")
    latent = latent[0]

    def other_core(value):
        return lax.ppermute(value, "core", [(0, 1), (1, 0)])

    def exchange(value):
        part = value.shape[-1]
        value = value.reshape(n_x * n_ep, -1, part)
        return lax.all_to_all(value, ("x", "ep"), split_axis=0, concat_axis=0, tiled=True)

    def shift(dx, dc):
        return [
            (2 * x + c, 2 * ((x + dx) % n_x) + (c ^ dc)) for x in range(n_x) for c in range(2)
        ]

    packed = jnp.transpose(attention_in[0], (1, 0, 2))
    pieces, blocks = [], []
    for dx in range(n_x):
        for dc in range(2):
            group = 2 * ((my_x + dx) % n_x) + (my_core ^ dc)
            piece = lax.dynamic_slice_in_dim(packed, group * group_width, group_width, axis=2)
            pieces.append(piece)
            if dx or dc:
                piece = lax.ppermute(piece, ("x", "core"), shift(dx, dc))
            blocks.append(piece)

    out_other = other_core(after(out_weight, pieces[1]))
    mine, given = attend(blocks)
    theirs = other_core(given)
    gate_mine, up_mine, down_mine = gate_weight[0], up_weight[0], down_weight[0]
    gate_other = other_core(after(gate_mine, theirs))
    up_other = other_core(after(up_mine, theirs))
    gates_up = (gate_mine, gate_other, up_mine, up_other)

    experts_count = 2 * n_ep
    capacity = max(2, 3 * tokens // experts_count)
    copies = n_x // 2
    n_cells = experts_count * capacity
    experts = route_experts[0]
    cells = ((experts % 2) * n_ep + experts // 2) * capacity + route_slots[0]
    row_cells = cells.T

    def dispatch(sent):
        part = sent.shape[1]
        sent = jnp.broadcast_to(
            sent.reshape(2, 1, n_ep, capacity, part), (2, copies, n_ep, capacity, part)
        )
        return exchange(sent).reshape(-1, part)

    residuals, stats = [], []
    for i, (own, *sends) in enumerate(project(mine, theirs, out_weight, out_other)):
        received = [
            lax.ppermute(value, "x", [(x, (x - dx) % n_x) for x in range(n_x)])
            for dx, value in enumerate(sends, 1)
        ]
        residual, stat = residual_part(latent, modulation, own, received, stats, i * width // 2)
        residuals.append(residual)
        stats.append(stat)
    down_other = other_core(after(down_mine, stats[1]))
    downs = (down_mine, down_other)

    quarter = width // 4
    rows, sums, token = None, (), stats[1]
    for start, stop in ((0, width - quarter), (width - quarter, width)):
        row = after(stats[1], token)
        token = pack(modulation, row_cells, n_cells, row, residuals, start, stop)
        rows = dispatch(token if rows is None else after(token, rows))
        sums = ffn_in(rows, gates_up, sums, start, stop == width)
    acts = sums

    out, token = None, acts
    for start, size in ((0, quarter), (quarter, width - quarter)):
        value = after(ffn_out(acts, downs, start, size), token)
        token = exchange(value)
        back = token.reshape(2, copies, n_ep * capacity, size)
        out = combine(residuals, modulation, cells, route_gates[0], back, start, out)
    return out[None]


def solution(mesh):
    n_sp, n_ep = mesh.devices.shape
    chips = Mesh(mesh.devices.reshape(n_sp // 2, 2, n_ep), ("x", "core", "ep"))
    sp = ("x", "core")
    return jax.shard_map(
        local,
        mesh=chips,
        in_specs=(
            P("ep", sp, None),
            P("ep", sp, None, None),
            P(sp, None),
            P(),
            P("ep", sp, None),
            P("ep", sp, None),
            P("ep", sp, None),
            P("ep", None, sp),
            P("ep", None, sp),
            P("ep", sp, None),
        ),
        out_specs=P("ep", sp, None),
        check_vma=False,
    )
```

```python
import functools
import math

import jax
import jax.numpy as jnp
from jax import lax
from jax.experimental import pallas as pl
from jax.experimental.pallas import tpu as pltpu
from jax.sharding import Mesh, PartitionSpec as P

HD = 128
VMEM = pl.BlockSpec(memory_space=pltpu.VMEM)
LOW = pl.CostEstimate(flops=1024, bytes_accessed=1024, transcendentals=0)


def dot32(a, b):
    return jnp.dot(a, b, preferred_element_type=jnp.float32)


def grant(mebibytes):
    return pltpu.CompilerParams(vmem_limit_bytes=mebibytes * 1024 * 1024)


def after(value, token):
    return lax.optimization_barrier((value, token))[0]


def attention_kernel(n_blocks, *refs):
    blocks = refs[:n_blocks]
    keep_ref, give_ref = refs[n_blocks:]
    tokens = keep_ref.shape[1]
    factor = math.log2(math.e) / math.sqrt(HD)
    for head in range(keep_ref.shape[-1] // HD):
        cols = slice(head * HD, (head + 1) * HD)
        queries, key_rows, value_rows = (
            jnp.concatenate([block[i, :, cols] for block in blocks], axis=0) for i in range(3)
        )
        scores = lax.dot_general(
            queries, key_rows, (((1,), (1,)), ((), ())), preferred_element_type=jnp.float32
        )
        lifted = jnp.exp2((scores - jnp.max(scores, axis=-1, keepdims=True)) * factor)
        total = jnp.sum(lifted, axis=-1, keepdims=True)
        mixed = (dot32(lifted.astype(jnp.bfloat16), value_rows) / total).astype(jnp.bfloat16)
        for i in range(n_blocks):
            out_ref = give_ref if i % 2 else keep_ref
            out_ref[i // 2, :, cols] = mixed[i * tokens : (i + 1) * tokens]


def attend(blocks):
    _, tokens, width = blocks[0].shape
    count = len(blocks)
    out = jax.ShapeDtypeStruct((count // 2, tokens, width), jnp.bfloat16)
    return pl.pallas_call(
        functools.partial(attention_kernel, count),
        out_shape=(out, out),
        in_specs=[VMEM] * count,
        out_specs=(VMEM, VMEM),
        compiler_params=grant(28),
        cost_estimate=LOW,
    )(*blocks)


def project_kernel(mine_ref, theirs_ref, mine_w, theirs_w, *refs):
    n_x, tokens, width = mine_ref.shape
    mine = mine_ref[...].reshape(n_x * tokens, width)
    theirs = theirs_ref[...].reshape(n_x * tokens, width)
    total = dot32(mine, mine_w[...]) + dot32(theirs, theirs_w[...])

    def write(outs):
        outs[0][...] = total[:tokens]
        for i, send_ref in enumerate(outs[1:], 1):
            send_ref[...] = total[i * tokens : (i + 1) * tokens].astype(jnp.bfloat16)

    half = pl.num_programs(0) // 2

    @pl.when(pl.program_id(0) < half)
    def _():
        write(refs[:n_x])

    @pl.when(pl.program_id(0) >= half)
    def _():
        write(refs[n_x:])


def project(mine, theirs, mine_w, theirs_w):
    n_x, tokens, depth = mine.shape
    width = mine_w.shape[1]
    tile = width // 4
    whole = pl.BlockSpec((n_x, tokens, depth), lambda n: (0, 0, 0))
    weight = pl.BlockSpec((depth, tile), lambda n: (0, n))
    out_shape, out_specs = [], []
    for place in (lambda n: (0, jnp.minimum(n, 1)), lambda n: (0, jnp.maximum(n - 2, 0))):
        for i in range(n_x):
            kind = jnp.bfloat16 if i else jnp.float32
            out_shape.append(jax.ShapeDtypeStruct((tokens, width // 2), kind))
            out_specs.append(pl.BlockSpec((tokens, tile), place))
    outs = pl.pallas_call(
        project_kernel,
        grid=(4,),
        out_shape=out_shape,
        in_specs=[whole, whole, weight, weight],
        out_specs=out_specs,
        compiler_params=grant(28),
        cost_estimate=LOW,
    )(mine, theirs, mine_w, theirs_w)
    return outs[:n_x], outs[n_x:]


def residual_kernel(start, n_recv, old_size, latent_ref, mod_ref, own_ref, *refs):
    recv_refs, old_refs = refs[:n_recv], refs[n_recv:-2]
    residual_ref, stats_ref = refs[-2:]
    size = own_ref.shape[1]
    cut = slice(start, start + size)
    projected = own_ref[...]
    for recv_ref in recv_refs:
        projected = projected + recv_ref[...].astype(jnp.float32)
    part = latent_ref[:, cut].astype(jnp.float32) + mod_ref[0:1, cut] * projected
    residual_ref[...] = part
    mean = jnp.mean(part, axis=-1, keepdims=True)
    centered = part - mean
    square = jnp.sum(centered * centered, axis=-1, keepdims=True)
    for old_ref in old_refs:
        old_mean, old_square = old_ref[:, 0:1], old_ref[:, 1:2]
        gap = old_mean - mean
        width = size + old_size
        mean = mean + gap * (old_size / width)
        square = square + old_square + gap * gap * (size * old_size / width)
        square = lax.rsqrt(square / width + 1e-06)
    stats_ref[:, 0:1] = mean
    stats_ref[:, 1:2] = square


def residual_part(latent, modulation, own, received, olds, start):
    tokens, size = own.shape
    return pl.pallas_call(
        functools.partial(residual_kernel, start, len(received), start),
        out_shape=[
            jax.ShapeDtypeStruct((tokens, size), jnp.float32),
            jax.ShapeDtypeStruct((tokens, 2), jnp.float32),
        ],
        in_specs=[VMEM] * (3 + len(received) + len(olds)),
        out_specs=[VMEM] * 2,
        compiler_params=grant(28),
        cost_estimate=LOW,
    )(latent, modulation, own, *received, *olds)


def pack_kernel(start, stop, mod_ref, cells_ref, stats_ref, *refs):
    *part_refs, sent_ref = refs
    tokens, size = part_refs[0].shape
    cells = lax.broadcasted_iota(jnp.int32, (sent_ref.shape[0], tokens), 0)
    one_hot = ((cells == cells_ref[0:1, :]) | (cells == cells_ref[1:2, :])).astype(jnp.bfloat16)
    for i, part_ref in enumerate(part_refs):
        low, high = max(start, i * size), min(stop, (i + 1) * size)
        if low < high:
            cut = slice(low, high)
            part = part_ref[:, low - i * size : high - i * size]
            normed = (part - stats_ref[:, 0:1]) * stats_ref[:, 1:2]
            moe_in = (normed * (1.0 + mod_ref[2:3, cut]) + mod_ref[1:2, cut]).astype(jnp.bfloat16)
            sent_ref[:, low - start : high - start] = dot32(one_hot, moe_in).astype(jnp.bfloat16)


def pack(modulation, cells, n_cells, stats, parts, start, stop):
    return pl.pallas_call(
        functools.partial(pack_kernel, start, stop),
        out_shape=jax.ShapeDtypeStruct((n_cells, stop - start), jnp.bfloat16),
        in_specs=[VMEM] * (3 + len(parts)),
        out_specs=VMEM,
        compiler_params=grant(28),
        cost_estimate=LOW,
    )(modulation, cells, stats, *parts)


def ffn_first_kernel(rows_ref, *refs):
    for weight, out_ref in zip(refs[:4], refs[4:]):
        out_ref[...] = dot32(rows_ref[...], weight[...])


def ffn_first(rows, weights):
    count, size = rows.shape
    units = weights[0].shape[1]
    tile = min(256, units)
    return pl.pallas_call(
        ffn_first_kernel,
        grid=(units // tile,),
        out_shape=[jax.ShapeDtypeStruct((count, units), jnp.float32)] * 4,
        in_specs=[pl.BlockSpec((count, size), lambda n: (0, 0))]
        + [pl.BlockSpec((size, tile), lambda n: (0, n))] * 4,
        out_specs=[pl.BlockSpec((count, tile), lambda n: (0, n))] * 4,
        compiler_params=grant(57),
        cost_estimate=LOW,
    )(rows, *weights)


def ffn_tail_kernel(head, rows_ref, *refs):
    weights, sums, downs = refs[:4], refs[4:8], refs[8:10]
    acts, value_ref = refs[10:12], refs[12]
    weight_buf, sum_buf, down_buf, sems = refs[13:]
    size = rows_ref.shape[1]
    low = weights[0].shape[0] - size
    order = (0, 2, 1, 3)
    copies = {}
    for i in order:
        copies["sum", i] = pltpu.make_async_copy(sums[i], sum_buf.at[i], sems.at[i])
        copies["weight", i] = pltpu.make_async_copy(
            weights[i].at[pl.ds(low, size), :], weight_buf.at[i], sems.at[4 + i]
        )
    for i in range(2):
        copies["down", i] = pltpu.make_async_copy(
            downs[i].at[:, pl.ds(0, head)], down_buf.at[i], sems.at[8 + i]
        )
    for copy in copies.values():
        copy.start()
    rows = rows_ref[...]

    def total(i):
        copies["sum", i].wait()
        copies["weight", i].wait()
        return dot32(rows, weight_buf[i]) + sum_buf[i]

    for i in range(2):
        gate = total(i)
        acts[i][...] = (gate / (1.0 + jnp.exp(-gate)) * total(2 + i)).astype(jnp.bfloat16)
    for i in range(2):
        copies["down", i].wait()
    value = dot32(acts[0][...], down_buf[0]) + dot32(acts[1][...], down_buf[1])
    value_ref[...] = value.astype(jnp.bfloat16)


def ffn_tail(rows, weights, sums, downs, head):
    count, size = rows.shape
    units = weights[0].shape[1]
    anywhere = pl.BlockSpec(memory_space=pl.ANY)
    act = jax.ShapeDtypeStruct((count, units), jnp.bfloat16)
    return pl.pallas_call(
        functools.partial(ffn_tail_kernel, head),
        out_shape=[act, act, jax.ShapeDtypeStruct((count, head), jnp.bfloat16)],
        in_specs=[VMEM] + [anywhere] * 10,
        out_specs=[VMEM] * 3,
        scratch_shapes=[
            pltpu.VMEM((4, size, units), jnp.bfloat16),
            pltpu.VMEM((4, count, units), jnp.float32),
            pltpu.VMEM((2, units, head), jnp.bfloat16),
            pltpu.SemaphoreType.DMA((10,)),
        ],
        compiler_params=grant(57),
        cost_estimate=LOW,
    )(rows, *weights, *sums, *downs)


def ffn_out_kernel(mine_ref, theirs_ref, mine_w, theirs_w, out_ref):
    total = dot32(mine_ref[...], mine_w[...]) + dot32(theirs_ref[...], theirs_w[...])
    out_ref[...] = total.astype(jnp.bfloat16)


def ffn_out(acts, weights, start, size):
    count, units = acts[0].shape
    tile = min(1024, size)
    first = start // tile
    act = pl.BlockSpec((count, units), lambda n: (0, 0))
    weight = pl.BlockSpec((units, tile), lambda n: (0, first + n))
    return pl.pallas_call(
        ffn_out_kernel,
        grid=(size // tile,),
        out_shape=jax.ShapeDtypeStruct((count, size), jnp.bfloat16),
        in_specs=[act, act, weight, weight],
        out_specs=pl.BlockSpec((count, tile), lambda n: (0, n)),
        compiler_params=grant(57),
        cost_estimate=LOW,
    )(*acts, *weights)


def combine_kernel(start, early_ref, late_ref, mod_ref, cells_ref, gates_ref, back_ref, *refs):
    *before, out_ref = refs
    tokens, part = early_ref.shape
    _, copies, half, size = back_ref.shape
    low = 0
    if before:
        low = start
        out_ref[:, :low] = before[0][...]
    cells = lax.broadcasted_iota(jnp.int32, (tokens, 2 * half), 1)
    one_hot = jnp.concatenate(
        [(cells == cells_ref[:, i : i + 1]).astype(jnp.bfloat16) for i in range(2)], axis=0
    )
    for ref, begin in ((early_ref, 0), (late_ref, part)):
        first, last = max(start, begin), min(start + size, begin + part)
        if first < last:
            picked = 0.0
            for i in range(copies):
                rows = back_ref[:, i, :, first - start : last - start]
                picked = picked + dot32(one_hot, rows.reshape(2 * half, last - first))
            combined = gates_ref[:, 0:1] * picked[:tokens] + gates_ref[:, 1:2] * picked[tokens:]
            total = ref[:, first - begin : last - begin] + mod_ref[3:4, first:last] * combined
            out_ref[:, first - start + low : last - start + low] = total.astype(jnp.bfloat16)


def combine(residuals, modulation, cells, gates, back, start, before):
    tokens = residuals[0].shape[0]
    size = back.shape[3] + sum(value.shape[1] for value in before)
    return pl.pallas_call(
        functools.partial(combine_kernel, start),
        out_shape=jax.ShapeDtypeStruct((tokens, size), jnp.bfloat16),
        in_specs=[VMEM] * (6 + len(before)),
        out_specs=VMEM,
        compiler_params=grant(28),
        cost_estimate=LOW,
    )(*residuals, modulation, cells, gates, back, *before)


def local(
    latent,
    attention_in,
    out_weight,
    modulation,
    route_experts,
    route_slots,
    route_gates,
    gate_weight,
    up_weight,
    down_weight,
):
    n_x = lax.axis_size("x")
    n_ep = lax.axis_size("ep")
    tokens = latent.shape[1]
    width = latent.shape[2]
    group_width = out_weight.shape[0]
    my_x = lax.axis_index("x")
    my_core = lax.axis_index("core")
    latent = latent[0]

    def other_core(value):
        return lax.ppermute(value, "core", [(0, 1), (1, 0)])

    def exchange(value):
        part = value.shape[-1]
        value = value.reshape(n_x * n_ep, -1, part)
        return lax.all_to_all(value, ("x", "ep"), split_axis=0, concat_axis=0, tiled=True)

    def shift(dx, dc):
        return [
            (2 * x + c, 2 * ((x + dx) % n_x) + (c ^ dc)) for x in range(n_x) for c in range(2)
        ]

    packed = jnp.transpose(attention_in[0], (1, 0, 2))
    pieces, blocks = [], []
    for dx in range(n_x):
        for dc in range(2):
            group = 2 * ((my_x + dx) % n_x) + (my_core ^ dc)
            piece = lax.dynamic_slice_in_dim(packed, group * group_width, group_width, axis=2)
            pieces.append(piece)
            if dx or dc:
                piece = lax.ppermute(piece, ("x", "core"), shift(dx, dc))
            blocks.append(piece)

    out_other = other_core(after(out_weight, pieces[1]))
    mine, given = attend(blocks)
    theirs = other_core(given)
    gate_mine, up_mine, down_mine = gate_weight[0], up_weight[0], down_weight[0]
    gate_other = other_core(after(gate_mine, theirs))
    up_other = other_core(after(up_mine, theirs))
    gates_up = (gate_mine, gate_other, up_mine, up_other)

    experts_count = 2 * n_ep
    capacity = max(2, 3 * tokens // experts_count)
    copies = n_x // 2
    n_cells = experts_count * capacity
    experts = route_experts[0]
    cells = ((experts % 2) * n_ep + experts // 2) * capacity + route_slots[0]
    row_cells = cells.T

    def dispatch(sent):
        part = sent.shape[1]
        sent = jnp.broadcast_to(
            sent.reshape(2, 1, n_ep, capacity, part), (2, copies, n_ep, capacity, part)
        )
        return exchange(sent).reshape(-1, part)

    residuals, stats = [], []
    for i, (own, *sends) in enumerate(project(mine, theirs, out_weight, out_other)):
        received = [
            lax.ppermute(value, "x", [(x, (x - dx) % n_x) for x in range(n_x)])
            for dx, value in enumerate(sends, 1)
        ]
        residual, stat = residual_part(latent, modulation, own, received, stats, i * width // 2)
        residuals.append(residual)
        stats.append(stat)
    down_other = other_core(after(down_mine, stats[1]))
    downs = (down_mine, down_other)

    quarter = width // 4
    sent = pack(modulation, row_cells, n_cells, stats[1], residuals, 0, width - quarter)
    rows = dispatch(sent)
    sums = ffn_first(rows, gates_up)
    sent = pack(
        modulation, row_cells, n_cells, after(stats[1], sent), residuals, width - quarter, width
    )
    rows = dispatch(after(sent, rows))
    *acts, value = ffn_tail(rows, gates_up, sums, downs, quarter)

    def give_back(value):
        return exchange(value).reshape(2, copies, n_ep * capacity, value.shape[1])

    gates = route_gates[0]
    back = give_back(value)
    done = combine(residuals, modulation, cells, gates, back, 0, [])
    back = give_back(after(ffn_out(acts, downs, quarter, width - quarter), back))
    out = combine(residuals, modulation, cells, gates, back, quarter, [done])
    return out[None]


def solution(mesh):
    n_sp, n_ep = mesh.devices.shape
    chips = Mesh(mesh.devices.reshape(n_sp // 2, 2, n_ep), ("x", "core", "ep"))
    sp = ("x", "core")
    return jax.shard_map(
        local,
        mesh=chips,
        in_specs=(
            P("ep", sp, None),
            P("ep", sp, None, None),
            P(sp, None),
            P(),
            P("ep", sp, None),
            P("ep", sp, None),
            P("ep", sp, None),
            P("ep", None, sp),
            P("ep", None, sp),
            P("ep", sp, None),
        ),
        out_specs=P("ep", sp, None),
        check_vma=False,
    )
```

```python
import functools
import math

import jax
import jax.numpy as jnp
from jax import lax
from jax.experimental import pallas as pl
from jax.experimental.pallas import tpu as pltpu
from jax.sharding import Mesh, PartitionSpec as P

HD = 128
VMEM = pl.BlockSpec(memory_space=pltpu.VMEM)
LOW = pl.CostEstimate(flops=1024, bytes_accessed=1024, transcendentals=0)


def dot32(a, b):
    return jnp.dot(a, b, preferred_element_type=jnp.float32)


def grant(mebibytes):
    return pltpu.CompilerParams(vmem_limit_bytes=mebibytes * 1024 * 1024)


def after(value, token):
    return lax.optimization_barrier((value, token))[0]


def attention_kernel(n_blocks, *refs):
    blocks = refs[:n_blocks]
    keep_ref, give_ref = refs[n_blocks:]
    tokens = keep_ref.shape[1]
    factor = math.log2(math.e) / math.sqrt(HD)
    for head in range(keep_ref.shape[-1] // HD):
        cols = slice(head * HD, (head + 1) * HD)
        queries, key_rows, value_rows = (
            jnp.concatenate([block[i, :, cols] for block in blocks], axis=0) for i in range(3)
        )
        scores = lax.dot_general(
            queries, key_rows, (((1,), (1,)), ((), ())), preferred_element_type=jnp.float32
        )
        lifted = jnp.exp2((scores - jnp.max(scores, axis=-1, keepdims=True)) * factor)
        total = jnp.sum(lifted, axis=-1, keepdims=True)
        mixed = (dot32(lifted.astype(jnp.bfloat16), value_rows) / total).astype(jnp.bfloat16)
        for i in range(n_blocks):
            out_ref = give_ref if i % 2 else keep_ref
            out_ref[i // 2, :, cols] = mixed[i * tokens : (i + 1) * tokens]


def attend(blocks):
    _, tokens, width = blocks[0].shape
    count = len(blocks)
    out = jax.ShapeDtypeStruct((count // 2, tokens, width), jnp.bfloat16)
    return pl.pallas_call(
        functools.partial(attention_kernel, count),
        out_shape=(out, out),
        in_specs=[VMEM] * count,
        out_specs=(VMEM, VMEM),
        compiler_params=grant(28),
        cost_estimate=LOW,
    )(*blocks)


def project_kernel(mine_ref, theirs_ref, mine_w, theirs_w, *refs):
    n_x, tokens, width = mine_ref.shape
    mine = mine_ref[...].reshape(n_x * tokens, width)
    theirs = theirs_ref[...].reshape(n_x * tokens, width)
    total = dot32(mine, mine_w[...]) + dot32(theirs, theirs_w[...])

    def write(outs):
        outs[0][...] = total[:tokens]
        for i, send_ref in enumerate(outs[1:], 1):
            send_ref[...] = total[i * tokens : (i + 1) * tokens].astype(jnp.bfloat16)

    half = pl.num_programs(0) // 2

    @pl.when(pl.program_id(0) < half)
    def _():
        write(refs[:n_x])

    @pl.when(pl.program_id(0) >= half)
    def _():
        write(refs[n_x:])


def project(mine, theirs, mine_w, theirs_w):
    n_x, tokens, depth = mine.shape
    width = mine_w.shape[1]
    tile = width // 4
    whole = pl.BlockSpec((n_x, tokens, depth), lambda n: (0, 0, 0))
    weight = pl.BlockSpec((depth, tile), lambda n: (0, n))
    out_shape, out_specs = [], []
    for place in (lambda n: (0, jnp.minimum(n, 1)), lambda n: (0, jnp.maximum(n - 2, 0))):
        for i in range(n_x):
            kind = jnp.bfloat16 if i else jnp.float32
            out_shape.append(jax.ShapeDtypeStruct((tokens, width // 2), kind))
            out_specs.append(pl.BlockSpec((tokens, tile), place))
    outs = pl.pallas_call(
        project_kernel,
        grid=(4,),
        out_shape=out_shape,
        in_specs=[whole, whole, weight, weight],
        out_specs=out_specs,
        compiler_params=grant(28),
        cost_estimate=LOW,
    )(mine, theirs, mine_w, theirs_w)
    return outs[:n_x], outs[n_x:]


def residual_kernel(start, n_recv, old_size, latent_ref, mod_ref, own_ref, *refs):
    recv_refs, old_refs = refs[:n_recv], refs[n_recv:-2]
    residual_ref, stats_ref = refs[-2:]
    size = own_ref.shape[1]
    cut = slice(start, start + size)
    projected = own_ref[...]
    for recv_ref in recv_refs:
        projected = projected + recv_ref[...].astype(jnp.float32)
    part = latent_ref[:, cut].astype(jnp.float32) + mod_ref[0:1, cut] * projected
    residual_ref[...] = part
    mean = jnp.mean(part, axis=-1, keepdims=True)
    centered = part - mean
    square = jnp.sum(centered * centered, axis=-1, keepdims=True)
    for old_ref in old_refs:
        old_mean, old_square = old_ref[:, 0:1], old_ref[:, 1:2]
        gap = old_mean - mean
        width = size + old_size
        mean = mean + gap * (old_size / width)
        square = square + old_square + gap * gap * (size * old_size / width)
        square = lax.rsqrt(square / width + 1e-06)
    stats_ref[:, 0:1] = mean
    stats_ref[:, 1:2] = square


def residual_part(latent, modulation, own, received, olds, start):
    tokens, size = own.shape
    return pl.pallas_call(
        functools.partial(residual_kernel, start, len(received), start),
        out_shape=[
            jax.ShapeDtypeStruct((tokens, size), jnp.float32),
            jax.ShapeDtypeStruct((tokens, 2), jnp.float32),
        ],
        in_specs=[VMEM] * (3 + len(received) + len(olds)),
        out_specs=[VMEM] * 2,
        compiler_params=grant(28),
        cost_estimate=LOW,
    )(latent, modulation, own, *received, *olds)


def pieces_of(start, stop, size, step):
    cuts = []
    low = start
    while low < stop:
        high = min(stop, low + step, (low // size + 1) * size)
        cuts.append((low, high))
        low = high
    return cuts


def pack_kernel(cuts, mod_ref, cells_ref, stats_ref, *refs):
    *part_refs, sent_ref, buf, sems = refs
    start = cuts[0][0]
    tokens, size = part_refs[0].shape
    cells = lax.broadcasted_iota(jnp.int32, (buf.shape[0], tokens), 0)
    one_hot = ((cells == cells_ref[0:1, :]) | (cells == cells_ref[1:2, :])).astype(jnp.bfloat16)
    copies = []
    for i, (low, high) in enumerate(cuts):
        cut = slice(low, high)
        begin = low // size * size
        part = part_refs[low // size][:, low - begin : high - begin]
        normed = (part - stats_ref[:, 0:1]) * stats_ref[:, 1:2]
        moe_in = (normed * (1.0 + mod_ref[2:3, cut]) + mod_ref[1:2, cut]).astype(jnp.bfloat16)
        place = pl.ds(low - start, high - low)
        buf[:, place] = dot32(one_hot, moe_in).astype(jnp.bfloat16)
        copies.append(
            pltpu.make_async_copy(buf.at[:, place], sent_ref.at[:, place], sems.at[i])
        )
        copies[-1].start()
    for copy in copies:
        copy.wait()


def pack(modulation, cells, n_cells, stats, parts, start, stop):
    cuts = pieces_of(start, stop, parts[0].shape[1], 1024)
    return pl.pallas_call(
        functools.partial(pack_kernel, cuts),
        out_shape=jax.ShapeDtypeStruct((n_cells, stop - start), jnp.bfloat16),
        in_specs=[VMEM] * (3 + len(parts)),
        out_specs=pl.BlockSpec(memory_space=pltpu.HBM),
        scratch_shapes=[
            pltpu.VMEM((n_cells, stop - start), jnp.bfloat16),
            pltpu.SemaphoreType.DMA((len(cuts),)),
        ],
        compiler_params=grant(28),
        cost_estimate=LOW,
    )(modulation, cells, stats, *parts)


def ffn_first_kernel(rows_ref, *refs):
    for weight, out_ref in zip(refs[:4], refs[4:]):
        out_ref[...] = dot32(rows_ref[...], weight[...])


def ffn_first(rows, weights):
    count, size = rows.shape
    units = weights[0].shape[1]
    tile = min(256, units)
    return pl.pallas_call(
        ffn_first_kernel,
        grid=(units // tile,),
        out_shape=[jax.ShapeDtypeStruct((count, units), jnp.float32)] * 4,
        in_specs=[pl.BlockSpec((count, size), lambda n: (0, 0))]
        + [pl.BlockSpec((size, tile), lambda n: (0, n))] * 4,
        out_specs=[pl.BlockSpec((count, tile), lambda n: (0, n))] * 4,
        compiler_params=grant(54),
        cost_estimate=LOW,
    )(rows, *weights)


def ffn_tail_kernel(head, rows_ref, *refs):
    weights, sums, downs = refs[:4], refs[4:8], refs[8:10]
    acts, value_ref = refs[10:12], refs[12]
    weight_buf, sum_buf, down_buf, sems = refs[13:]
    size = rows_ref.shape[1]
    low = weights[0].shape[0] - size
    order = (0, 2, 1, 3)
    copies = {}
    for i in order:
        copies["sum", i] = pltpu.make_async_copy(sums[i], sum_buf.at[i], sems.at[i])
        copies["weight", i] = pltpu.make_async_copy(
            weights[i].at[pl.ds(low, size), :], weight_buf.at[i], sems.at[4 + i]
        )
    for i in range(2):
        copies["down", i] = pltpu.make_async_copy(
            downs[i].at[:, pl.ds(0, head)], down_buf.at[i], sems.at[8 + i]
        )
    for copy in copies.values():
        copy.start()
    rows = rows_ref[...]

    def total(i):
        copies["sum", i].wait()
        copies["weight", i].wait()
        return dot32(rows, weight_buf[i]) + sum_buf[i]

    for i in range(2):
        gate = total(i)
        acts[i][...] = (gate / (1.0 + jnp.exp(-gate)) * total(2 + i)).astype(jnp.bfloat16)
    for i in range(2):
        copies["down", i].wait()
    value = dot32(acts[0][...], down_buf[0]) + dot32(acts[1][...], down_buf[1])
    value_ref[...] = value.astype(jnp.bfloat16)


def ffn_tail(rows, weights, sums, downs, head):
    count, size = rows.shape
    units = weights[0].shape[1]
    anywhere = pl.BlockSpec(memory_space=pl.ANY)
    act = jax.ShapeDtypeStruct((count, units), jnp.bfloat16)
    return pl.pallas_call(
        functools.partial(ffn_tail_kernel, head),
        out_shape=[act, act, jax.ShapeDtypeStruct((count, head), jnp.bfloat16)],
        in_specs=[VMEM] + [anywhere] * 10,
        out_specs=[VMEM] * 3,
        scratch_shapes=[
            pltpu.VMEM((4, size, units), jnp.bfloat16),
            pltpu.VMEM((4, count, units), jnp.float32),
            pltpu.VMEM((2, units, head), jnp.bfloat16),
            pltpu.SemaphoreType.DMA((10,)),
        ],
        compiler_params=grant(54),
        cost_estimate=LOW,
    )(rows, *weights, *sums, *downs)


def ffn_out_kernel(mine_ref, theirs_ref, mine_w, theirs_w, out_ref):
    total = dot32(mine_ref[...], mine_w[...]) + dot32(theirs_ref[...], theirs_w[...])
    out_ref[...] = total.astype(jnp.bfloat16)


def ffn_out(acts, weights, start, size):
    count, units = acts[0].shape
    tile = min(1024, size)
    first = start // tile
    act = pl.BlockSpec((count, units), lambda n: (0, 0))
    weight = pl.BlockSpec((units, tile), lambda n: (0, first + n))
    return pl.pallas_call(
        ffn_out_kernel,
        grid=(size // tile,),
        out_shape=jax.ShapeDtypeStruct((count, size), jnp.bfloat16),
        in_specs=[act, act, weight, weight],
        out_specs=pl.BlockSpec((count, tile), lambda n: (0, n)),
        compiler_params=grant(57),
        cost_estimate=LOW,
    )(*acts, *weights)


def combine_kernel(cuts, early_ref, late_ref, mod_ref, cells_ref, gates_ref, back_ref, *refs):
    *before, out_ref, back_buf, out_buf, load_sems, store_sems = refs
    tokens, part = early_ref.shape
    _, copies, half, _ = back_ref.shape
    start = cuts[0][0]
    shift = start if before else 0
    loads, stores = [], []
    for i, (low, high) in enumerate(cuts):
        place = pl.ds(low - start, high - low)
        loads.append(
            pltpu.make_async_copy(
                back_ref.at[:, :, :, place], back_buf.at[:, :, :, place], load_sems.at[i]
            )
        )
        loads[-1].start()
    if before:
        place = pl.ds(0, shift)
        stores.append(
            pltpu.make_async_copy(before[0], out_ref.at[:, place], store_sems.at[len(cuts)])
        )
        stores[-1].start()
    cells = lax.broadcasted_iota(jnp.int32, (tokens, 2 * half), 1)
    one_hot = jnp.concatenate(
        [(cells == cells_ref[:, i : i + 1]).astype(jnp.bfloat16) for i in range(2)], axis=0
    )
    for i, (low, high) in enumerate(cuts):
        loads[i].wait()
        picked = 0.0
        for j in range(copies):
            rows = back_buf[:, j, :, low - start : high - start]
            picked = picked + dot32(one_hot, rows.reshape(2 * half, high - low))
        combined = gates_ref[:, 0:1] * picked[:tokens] + gates_ref[:, 1:2] * picked[tokens:]
        ref = late_ref if low >= part else early_ref
        begin = low // part * part
        total = ref[:, low - begin : high - begin] + mod_ref[3:4, low:high] * combined
        place = pl.ds(low - start, high - low)
        out_buf[:, place] = total.astype(jnp.bfloat16)
        target = pl.ds(low - start + shift, high - low)
        stores.append(
            pltpu.make_async_copy(out_buf.at[:, place], out_ref.at[:, target], store_sems.at[i])
        )
        stores[-1].start()
    for store in stores:
        store.wait()


def combine(residuals, modulation, cells, gates, back, start, before):
    tokens, part = residuals[0].shape
    size = back.shape[3]
    cuts = pieces_of(start, start + size, part, 1024)
    width = size + sum(value.shape[1] for value in before)
    return pl.pallas_call(
        functools.partial(combine_kernel, cuts),
        out_shape=jax.ShapeDtypeStruct((tokens, width), jnp.bfloat16),
        in_specs=[VMEM] * 5 + [pl.BlockSpec(memory_space=pl.ANY)] + [VMEM] * len(before),
        out_specs=pl.BlockSpec(memory_space=pl.ANY),
        scratch_shapes=[
            pltpu.VMEM(back.shape, jnp.bfloat16),
            pltpu.VMEM((tokens, size), jnp.bfloat16),
            pltpu.SemaphoreType.DMA((len(cuts),)),
            pltpu.SemaphoreType.DMA((len(cuts) + 1,)),
        ],
        compiler_params=grant(28),
        cost_estimate=LOW,
    )(*residuals, modulation, cells, gates, back, *before)


def local(
    latent,
    attention_in,
    out_weight,
    modulation,
    route_experts,
    route_slots,
    route_gates,
    gate_weight,
    up_weight,
    down_weight,
):
    n_x = lax.axis_size("x")
    n_ep = lax.axis_size("ep")
    tokens = latent.shape[1]
    width = latent.shape[2]
    group_width = out_weight.shape[0]
    my_x = lax.axis_index("x")
    my_core = lax.axis_index("core")
    latent = latent[0]

    def other_core(value):
        return lax.ppermute(value, "core", [(0, 1), (1, 0)])

    def exchange(value):
        part = value.shape[-1]
        value = value.reshape(n_x * n_ep, -1, part)
        return lax.all_to_all(value, ("x", "ep"), split_axis=0, concat_axis=0, tiled=True)

    def shift(dx, dc):
        return [
            (2 * x + c, 2 * ((x + dx) % n_x) + (c ^ dc)) for x in range(n_x) for c in range(2)
        ]

    packed = jnp.transpose(attention_in[0], (1, 0, 2))
    pieces, blocks = [], []
    for dx in range(n_x):
        for dc in range(2):
            group = 2 * ((my_x + dx) % n_x) + (my_core ^ dc)
            piece = lax.dynamic_slice_in_dim(packed, group * group_width, group_width, axis=2)
            pieces.append(piece)
            if dx or dc:
                piece = lax.ppermute(piece, ("x", "core"), shift(dx, dc))
            blocks.append(piece)

    out_other = other_core(after(out_weight, pieces[1]))
    mine, given = attend(blocks)
    theirs = other_core(given)
    gate_mine, up_mine, down_mine = gate_weight[0], up_weight[0], down_weight[0]
    gate_other = other_core(after(gate_mine, theirs))
    up_other = other_core(after(up_mine, theirs))
    gates_up = (gate_mine, gate_other, up_mine, up_other)

    experts_count = 2 * n_ep
    capacity = max(2, 3 * tokens // experts_count)
    copies = n_x // 2
    n_cells = experts_count * capacity
    experts = route_experts[0]
    cells = ((experts % 2) * n_ep + experts // 2) * capacity + route_slots[0]
    row_cells = cells.T

    def dispatch(sent):
        part = sent.shape[1]
        sent = jnp.broadcast_to(
            sent.reshape(2, 1, n_ep, capacity, part), (2, copies, n_ep, capacity, part)
        )
        return exchange(sent).reshape(-1, part)

    residuals, stats = [], []
    for i, (own, *sends) in enumerate(project(mine, theirs, out_weight, out_other)):
        received = [
            lax.ppermute(value, "x", [(x, (x - dx) % n_x) for x in range(n_x)])
            for dx, value in enumerate(sends, 1)
        ]
        residual, stat = residual_part(latent, modulation, own, received, stats, i * width // 2)
        residuals.append(residual)
        stats.append(stat)
    down_other = other_core(after(down_mine, stats[1]))
    downs = (down_mine, down_other)

    quarter = width // 4
    sent = pack(modulation, row_cells, n_cells, stats[1], residuals, 0, width - quarter)
    rows = dispatch(sent)
    sums = ffn_first(rows, gates_up)
    sent = pack(
        modulation, row_cells, n_cells, after(stats[1], sent), residuals, width - quarter, width
    )
    rows = dispatch(after(sent, rows))
    *acts, value = ffn_tail(rows, gates_up, sums, downs, quarter)

    def give_back(value):
        return exchange(value).reshape(2, copies, n_ep * capacity, value.shape[1])

    gates = route_gates[0]
    back = give_back(value)
    done = combine(residuals, modulation, cells, gates, back, 0, [])
    back = give_back(after(ffn_out(acts, downs, quarter, width - quarter), back))
    out = combine(residuals, modulation, cells, gates, back, quarter, [done])
    return out[None]


def solution(mesh):
    n_sp, n_ep = mesh.devices.shape
    chips = Mesh(mesh.devices.reshape(n_sp // 2, 2, n_ep), ("x", "core", "ep"))
    sp = ("x", "core")
    return jax.shard_map(
        local,
        mesh=chips,
        in_specs=(
            P("ep", sp, None),
            P("ep", sp, None, None),
            P(sp, None),
            P(),
            P("ep", sp, None),
            P("ep", sp, None),
            P("ep", sp, None),
            P("ep", None, sp),
            P("ep", None, sp),
            P("ep", sp, None),
        ),
        out_specs=P("ep", sp, None),
        check_vma=False,
    )
```

```python
import functools
import math

import jax
import jax.numpy as jnp
from jax import lax
from jax.experimental import pallas as pl
from jax.experimental.pallas import tpu as pltpu
from jax.sharding import Mesh, PartitionSpec as P

HD = 128
VMEM = pl.BlockSpec(memory_space=pltpu.VMEM)
LOW = pl.CostEstimate(flops=1024, bytes_accessed=1024, transcendentals=0)


def dot32(a, b):
    return jnp.dot(a, b, preferred_element_type=jnp.float32)


def grant(mebibytes):
    return pltpu.CompilerParams(vmem_limit_bytes=mebibytes * 1024 * 1024)


def after(value, token):
    return lax.optimization_barrier((value, token))[0]


def attention_kernel(n_blocks, *refs):
    blocks = refs[:n_blocks]
    keep_ref, give_ref = refs[n_blocks:]
    tokens = keep_ref.shape[1]
    factor = math.log2(math.e) / math.sqrt(HD)
    for head in range(keep_ref.shape[-1] // HD):
        cols = slice(head * HD, (head + 1) * HD)
        queries, key_rows, value_rows = (
            jnp.concatenate([block[i, :, cols] for block in blocks], axis=0) for i in range(3)
        )
        scores = lax.dot_general(
            queries, key_rows, (((1,), (1,)), ((), ())), preferred_element_type=jnp.float32
        )
        lifted = jnp.exp2((scores - jnp.max(scores, axis=-1, keepdims=True)) * factor)
        total = jnp.sum(lifted, axis=-1, keepdims=True)
        mixed = (dot32(lifted.astype(jnp.bfloat16), value_rows) / total).astype(jnp.bfloat16)
        for i in range(n_blocks):
            out_ref = give_ref if i % 2 else keep_ref
            out_ref[i // 2, :, cols] = mixed[i * tokens : (i + 1) * tokens]


def attend(blocks):
    _, tokens, width = blocks[0].shape
    count = len(blocks)
    out = jax.ShapeDtypeStruct((count // 2, tokens, width), jnp.bfloat16)
    return pl.pallas_call(
        functools.partial(attention_kernel, count),
        out_shape=(out, out),
        in_specs=[VMEM] * count,
        out_specs=(VMEM, VMEM),
        compiler_params=grant(28),
        cost_estimate=LOW,
    )(*blocks)


def project_kernel(mine_ref, theirs_ref, mine_w, theirs_w, *refs):
    n_x, tokens, width = mine_ref.shape
    mine = mine_ref[...].reshape(n_x * tokens, width)
    theirs = theirs_ref[...].reshape(n_x * tokens, width)
    total = dot32(mine, mine_w[...]) + dot32(theirs, theirs_w[...])

    def write(outs):
        outs[0][...] = total[:tokens]
        for i, send_ref in enumerate(outs[1:], 1):
            send_ref[...] = total[i * tokens : (i + 1) * tokens].astype(jnp.bfloat16)

    half = pl.num_programs(0) // 2

    @pl.when(pl.program_id(0) < half)
    def _():
        write(refs[:n_x])

    @pl.when(pl.program_id(0) >= half)
    def _():
        write(refs[n_x:])


def project(mine, theirs, mine_w, theirs_w):
    n_x, tokens, depth = mine.shape
    width = mine_w.shape[1]
    tile = width // 4
    whole = pl.BlockSpec((n_x, tokens, depth), lambda n: (0, 0, 0))
    weight = pl.BlockSpec((depth, tile), lambda n: (0, n))
    out_shape, out_specs = [], []
    for place in (lambda n: (0, jnp.minimum(n, 1)), lambda n: (0, jnp.maximum(n - 2, 0))):
        for i in range(n_x):
            kind = jnp.bfloat16 if i else jnp.float32
            out_shape.append(jax.ShapeDtypeStruct((tokens, width // 2), kind))
            out_specs.append(pl.BlockSpec((tokens, tile), place))
    outs = pl.pallas_call(
        project_kernel,
        grid=(4,),
        out_shape=out_shape,
        in_specs=[whole, whole, weight, weight],
        out_specs=out_specs,
        compiler_params=grant(28),
        cost_estimate=LOW,
    )(mine, theirs, mine_w, theirs_w)
    return outs[:n_x], outs[n_x:]


def residual_kernel(start, n_recv, old_size, latent_ref, mod_ref, own_ref, *refs):
    recv_refs, old_refs = refs[:n_recv], refs[n_recv:-2]
    residual_ref, stats_ref = refs[-2:]
    size = own_ref.shape[1]
    cut = slice(start, start + size)
    projected = own_ref[...]
    for recv_ref in recv_refs:
        projected = projected + recv_ref[...].astype(jnp.float32)
    part = latent_ref[:, cut].astype(jnp.float32) + mod_ref[0:1, cut] * projected
    residual_ref[...] = part
    mean = jnp.mean(part, axis=-1, keepdims=True)
    centered = part - mean
    square = jnp.sum(centered * centered, axis=-1, keepdims=True)
    for old_ref in old_refs:
        old_mean, old_square = old_ref[:, 0:1], old_ref[:, 1:2]
        gap = old_mean - mean
        width = size + old_size
        mean = mean + gap * (old_size / width)
        square = square + old_square + gap * gap * (size * old_size / width)
        square = lax.rsqrt(square / width + 1e-06)
    stats_ref[:, 0:1] = mean
    stats_ref[:, 1:2] = square


def residual_part(latent, modulation, own, received, olds, start):
    tokens, size = own.shape
    return pl.pallas_call(
        functools.partial(residual_kernel, start, len(received), start),
        out_shape=[
            jax.ShapeDtypeStruct((tokens, size), jnp.float32),
            jax.ShapeDtypeStruct((tokens, 2), jnp.float32),
        ],
        in_specs=[VMEM] * (3 + len(received) + len(olds)),
        out_specs=[VMEM] * 2,
        compiler_params=grant(28),
        cost_estimate=LOW,
    )(latent, modulation, own, *received, *olds)


def pieces_of(start, stop, size, step):
    cuts = []
    low = start
    while low < stop:
        high = min(stop, low + step, (low // size + 1) * size)
        cuts.append((low, high))
        low = high
    return cuts


def pack_kernel(start, stop, mod_ref, cells_ref, stats_ref, *refs):
    *part_refs, sent_ref = refs
    tokens, size = part_refs[0].shape
    cells = lax.broadcasted_iota(jnp.int32, (sent_ref.shape[0], tokens), 0)
    one_hot = ((cells == cells_ref[0:1, :]) | (cells == cells_ref[1:2, :])).astype(jnp.bfloat16)
    for i, part_ref in enumerate(part_refs):
        low, high = max(start, i * size), min(stop, (i + 1) * size)
        if low < high:
            cut = slice(low, high)
            part = part_ref[:, low - i * size : high - i * size]
            normed = (part - stats_ref[:, 0:1]) * stats_ref[:, 1:2]
            moe_in = (normed * (1.0 + mod_ref[2:3, cut]) + mod_ref[1:2, cut]).astype(jnp.bfloat16)
            sent_ref[:, low - start : high - start] = dot32(one_hot, moe_in).astype(jnp.bfloat16)


def pack(modulation, cells, n_cells, stats, parts, start, stop):
    return pl.pallas_call(
        functools.partial(pack_kernel, start, stop),
        out_shape=jax.ShapeDtypeStruct((n_cells, stop - start), jnp.bfloat16),
        in_specs=[VMEM] * (3 + len(parts)),
        out_specs=VMEM,
        compiler_params=grant(28),
        cost_estimate=LOW,
    )(modulation, cells, stats, *parts)


def ffn_first_kernel(rows_ref, *refs):
    for weight, out_ref in zip(refs[:4], refs[4:]):
        out_ref[...] = dot32(rows_ref[...], weight[...])


def ffn_first(rows, weights):
    count, size = rows.shape
    units = weights[0].shape[1]
    tile = min(256, units)
    return pl.pallas_call(
        ffn_first_kernel,
        grid=(units // tile,),
        out_shape=[jax.ShapeDtypeStruct((count, units), jnp.float32)] * 4,
        in_specs=[pl.BlockSpec((count, size), lambda n: (0, 0))]
        + [pl.BlockSpec((size, tile), lambda n: (0, n))] * 4,
        out_specs=[pl.BlockSpec((count, tile), lambda n: (0, n))] * 4,
        compiler_params=grant(54),
        cost_estimate=LOW,
    )(rows, *weights)


def ffn_tail_kernel(head, rows_ref, *refs):
    weights, sums, downs = refs[:4], refs[4:8], refs[8:10]
    acts, value_ref = refs[10:12], refs[12]
    weight_buf, sum_buf, down_buf, sems = refs[13:]
    size = rows_ref.shape[1]
    low = weights[0].shape[0] - size
    copies = {}
    for i in (0, 2, 1, 3):
        copies["sum", i] = pltpu.make_async_copy(sums[i], sum_buf.at[i], sems.at[i])
        copies["weight", i] = pltpu.make_async_copy(
            weights[i].at[pl.ds(low, size), :], weight_buf.at[i], sems.at[4 + i]
        )
        if i >= 2:
            copies["down", i - 2] = pltpu.make_async_copy(
                downs[i - 2].at[:, pl.ds(0, head)], down_buf.at[i - 2], sems.at[6 + i]
            )
    for copy in copies.values():
        copy.start()
    rows = rows_ref[...]

    def total(i):
        copies["sum", i].wait()
        copies["weight", i].wait()
        return dot32(rows, weight_buf[i]) + sum_buf[i]

    value = 0.0
    for i in range(2):
        gate = total(i)
        acts[i][...] = (gate / (1.0 + jnp.exp(-gate)) * total(2 + i)).astype(jnp.bfloat16)
        copies["down", i].wait()
        value = value + dot32(acts[i][...], down_buf[i])
    value_ref[...] = value.astype(jnp.bfloat16)


def ffn_tail(rows, weights, sums, downs, head):
    count, size = rows.shape
    units = weights[0].shape[1]
    anywhere = pl.BlockSpec(memory_space=pl.ANY)
    act = jax.ShapeDtypeStruct((count, units), jnp.bfloat16)
    return pl.pallas_call(
        functools.partial(ffn_tail_kernel, head),
        out_shape=[act, act, jax.ShapeDtypeStruct((count, head), jnp.bfloat16)],
        in_specs=[VMEM] + [anywhere] * 10,
        out_specs=[VMEM] * 3,
        scratch_shapes=[
            pltpu.VMEM((4, size, units), jnp.bfloat16),
            pltpu.VMEM((4, count, units), jnp.float32),
            pltpu.VMEM((2, units, head), jnp.bfloat16),
            pltpu.SemaphoreType.DMA((10,)),
        ],
        compiler_params=grant(54),
        cost_estimate=LOW,
    )(rows, *weights, *sums, *downs)


def ffn_out_kernel(mine_ref, theirs_ref, mine_w, theirs_w, out_ref):
    total = dot32(mine_ref[...], mine_w[...]) + dot32(theirs_ref[...], theirs_w[...])
    out_ref[...] = total.astype(jnp.bfloat16)


def ffn_out(acts, weights, start, size):
    count, units = acts[0].shape
    tile = min(1024, size)
    first = start // tile
    act = pl.BlockSpec((count, units), lambda n: (0, 0))
    weight = pl.BlockSpec((units, tile), lambda n: (0, first + n))
    return pl.pallas_call(
        ffn_out_kernel,
        grid=(size // tile,),
        out_shape=jax.ShapeDtypeStruct((count, size), jnp.bfloat16),
        in_specs=[act, act, weight, weight],
        out_specs=pl.BlockSpec((count, tile), lambda n: (0, n)),
        compiler_params=grant(57),
        cost_estimate=LOW,
    )(*acts, *weights)


def combine_kernel(cuts, early_ref, late_ref, mod_ref, cells_ref, gates_ref, back_ref, *refs):
    *before, out_ref, back_buf, out_buf, load_sems, store_sems = refs
    tokens, part = early_ref.shape
    _, copies, half, _ = back_ref.shape
    start = cuts[0][0]
    shift = start if before else 0
    loads, stores = [], []
    for i, (low, high) in enumerate(cuts):
        place = pl.ds(low - start, high - low)
        loads.append(
            pltpu.make_async_copy(
                back_ref.at[:, :, :, place], back_buf.at[:, :, :, place], load_sems.at[i]
            )
        )
        loads[-1].start()
    if before:
        place = pl.ds(0, shift)
        stores.append(
            pltpu.make_async_copy(before[0], out_ref.at[:, place], store_sems.at[len(cuts)])
        )
        stores[-1].start()
    cells = lax.broadcasted_iota(jnp.int32, (tokens, 2 * half), 1)
    one_hot = jnp.concatenate(
        [(cells == cells_ref[:, i : i + 1]).astype(jnp.bfloat16) for i in range(2)], axis=0
    )
    for i, (low, high) in enumerate(cuts):
        loads[i].wait()
        picked = 0.0
        for j in range(copies):
            rows = back_buf[:, j, :, low - start : high - start]
            picked = picked + dot32(one_hot, rows.reshape(2 * half, high - low))
        combined = gates_ref[:, 0:1] * picked[:tokens] + gates_ref[:, 1:2] * picked[tokens:]
        ref = late_ref if low >= part else early_ref
        begin = low // part * part
        total = ref[:, low - begin : high - begin] + mod_ref[3:4, low:high] * combined
        place = pl.ds(low - start, high - low)
        out_buf[:, place] = total.astype(jnp.bfloat16)
        target = pl.ds(low - start + shift, high - low)
        stores.append(
            pltpu.make_async_copy(out_buf.at[:, place], out_ref.at[:, target], store_sems.at[i])
        )
        stores[-1].start()
    for store in stores:
        store.wait()


def combine(residuals, modulation, cells, gates, back, start, before):
    tokens, part = residuals[0].shape
    size = back.shape[3]
    cuts = pieces_of(start, start + size, part, 1024)
    width = size + sum(value.shape[1] for value in before)
    return pl.pallas_call(
        functools.partial(combine_kernel, cuts),
        out_shape=jax.ShapeDtypeStruct((tokens, width), jnp.bfloat16),
        in_specs=[VMEM] * 5 + [pl.BlockSpec(memory_space=pl.ANY)] + [VMEM] * len(before),
        out_specs=pl.BlockSpec(memory_space=pl.ANY),
        scratch_shapes=[
            pltpu.VMEM(back.shape, jnp.bfloat16),
            pltpu.VMEM((tokens, size), jnp.bfloat16),
            pltpu.SemaphoreType.DMA((len(cuts),)),
            pltpu.SemaphoreType.DMA((len(cuts) + 1,)),
        ],
        compiler_params=grant(28),
        cost_estimate=LOW,
    )(*residuals, modulation, cells, gates, back, *before)


def local(
    latent,
    attention_in,
    out_weight,
    modulation,
    route_experts,
    route_slots,
    route_gates,
    gate_weight,
    up_weight,
    down_weight,
):
    n_x = lax.axis_size("x")
    n_ep = lax.axis_size("ep")
    tokens = latent.shape[1]
    width = latent.shape[2]
    group_width = out_weight.shape[0]
    my_x = lax.axis_index("x")
    my_core = lax.axis_index("core")
    latent = latent[0]

    def other_core(value):
        return lax.ppermute(value, "core", [(0, 1), (1, 0)])

    def exchange(value):
        part = value.shape[-1]
        value = value.reshape(n_x * n_ep, -1, part)
        return lax.all_to_all(value, ("x", "ep"), split_axis=0, concat_axis=0, tiled=True)

    def shift(dx, dc):
        return [
            (2 * x + c, 2 * ((x + dx) % n_x) + (c ^ dc)) for x in range(n_x) for c in range(2)
        ]

    packed = jnp.transpose(attention_in[0], (1, 0, 2))
    pieces, blocks = [], []
    for dx in range(n_x):
        for dc in range(2):
            group = 2 * ((my_x + dx) % n_x) + (my_core ^ dc)
            piece = lax.dynamic_slice_in_dim(packed, group * group_width, group_width, axis=2)
            pieces.append(piece)
            if dx or dc:
                piece = lax.ppermute(piece, ("x", "core"), shift(dx, dc))
            blocks.append(piece)

    out_other = other_core(after(out_weight, pieces[1]))
    mine, given = attend(blocks)
    theirs = other_core(given)
    gate_mine, up_mine, down_mine = gate_weight[0], up_weight[0], down_weight[0]
    gate_other = other_core(after(gate_mine, theirs))
    up_other = other_core(after(up_mine, theirs))
    gates_up = (gate_mine, gate_other, up_mine, up_other)

    experts_count = 2 * n_ep
    capacity = max(2, 3 * tokens // experts_count)
    copies = n_x // 2
    n_cells = experts_count * capacity
    experts = route_experts[0]
    cells = ((experts % 2) * n_ep + experts // 2) * capacity + route_slots[0]
    row_cells = cells.T

    def dispatch(sent):
        part = sent.shape[1]
        sent = jnp.broadcast_to(
            sent.reshape(2, 1, n_ep, capacity, part), (2, copies, n_ep, capacity, part)
        )
        return exchange(sent).reshape(-1, part)

    residuals, stats = [], []
    for i, (own, *sends) in enumerate(project(mine, theirs, out_weight, out_other)):
        received = [
            lax.ppermute(value, "x", [(x, (x - dx) % n_x) for x in range(n_x)])
            for dx, value in enumerate(sends, 1)
        ]
        residual, stat = residual_part(latent, modulation, own, received, stats, i * width // 2)
        residuals.append(residual)
        stats.append(stat)
    down_other = other_core(after(down_mine, stats[1]))
    downs = (down_mine, down_other)

    quarter = width // 4
    sent = pack(modulation, row_cells, n_cells, stats[1], residuals, 0, width - quarter)
    rows = dispatch(sent)
    sums = ffn_first(rows, gates_up)
    sent = pack(
        modulation, row_cells, n_cells, after(stats[1], sent), residuals, width - quarter, width
    )
    rows = dispatch(after(sent, rows))
    *acts, value = ffn_tail(rows, gates_up, sums, downs, quarter)

    def give_back(value):
        return exchange(value).reshape(2, copies, n_ep * capacity, value.shape[1])

    gates = route_gates[0]
    back = give_back(value)
    done = combine(residuals, modulation, cells, gates, back, 0, [])
    back = give_back(after(ffn_out(acts, downs, quarter, width - quarter), back))
    out = combine(residuals, modulation, cells, gates, back, quarter, [done])
    return out[None]


def solution(mesh):
    n_sp, n_ep = mesh.devices.shape
    chips = Mesh(mesh.devices.reshape(n_sp // 2, 2, n_ep), ("x", "core", "ep"))
    sp = ("x", "core")
    return jax.shard_map(
        local,
        mesh=chips,
        in_specs=(
            P("ep", sp, None),
            P("ep", sp, None, None),
            P(sp, None),
            P(),
            P("ep", sp, None),
            P("ep", sp, None),
            P("ep", sp, None),
            P("ep", None, sp),
            P("ep", None, sp),
            P("ep", sp, None),
        ),
        out_specs=P("ep", sp, None),
        check_vma=False,
    )
```
